128 devices in a mesh: pos: 16 (over x, z), tile: 8 (over y, core).
Axes of the slice: x: 4, y: 4, z: 4, core: 2. Of those that a mesh axis runs over, the one named last changes fastest.
Arguments:
- object_field: float32 [2, 2048, 8192], P(None, 'tile', 'pos'), may hold values from -6 to 6
- probe_field: float32 [2, 256, 256], replicated, may hold values from -6 to 6
- measured: float32 [2048, 256, 256], P(('pos', 'tile')), may hold values from 0.5 to 2.5
- offsets: int32 [2048, 2], P(('pos', 'tile')), may hold values from -128 to 8063, as said below
Outputs:
- object_grad: float32 [2, 2048, 8192], P(None, 'tile', 'pos')
- probe_grad: float32 [2, 256, 256], replicated
The draws below stay inside these ranges and needn't reach their ends.
Inputs may be any that keep to these rules, and one draw needn't show every extreme that they name: `offsets`: position n belongs to device slab n // 16 = p * 8 + t; its patch centre (r + 128, c + 128) lies in tile rows t * 256 to t * 256 + 255 and tile columns p * 512 to p * 512 + 511.
All inputs are finite; a program needn't handle non-finite values.
Results may differ from the reference program's by a relative error of at most 0.0003.
Values sent between devices are 32-bit elements; how exact they have to be, the bound alone decides.
A program may use at most 128 MiB of HBM per device.

```python
import jax
import jax.numpy as jnp
from jax import lax

PROBE = 256
TR = 256
TC = 512
POS_DEV = 16
OBJ_R = 2048
OBJ_C = 8192
POSITIONS = 2048
N_TILE = 8


def draw_offsets(key, part):
    key = jax.random.fold_in(key, 7)
    key_rows, key_cols = jax.random.split(key)
    position_index = jnp.arange(POSITIONS, dtype=jnp.int32)
    device = position_index // POS_DEV
    group_index = device // N_TILE
    tile_index = device % N_TILE
    row_pick = jax.random.randint(key_rows, (POSITIONS,), 0, TR)
    col_pick = jax.random.randint(key_cols, (POSITIONS,), 0, TC)
    first_one = position_index == 0
    last_one = position_index == POSITIONS - 1
    row_pick = jnp.where(first_one, 0, jnp.where(last_one, TR - 1, row_pick))
    col_pick = jnp.where(first_one, 0, jnp.where(last_one, TC - 1, col_pick))
    row_top = tile_index * TR + row_pick - PROBE // 2
    col_top = group_index * TC + col_pick - PROBE // 2
    return jnp.stack([row_top, col_top], axis=1).astype(jnp.int32)


def steps_of(own_key, extent, cuts, low, high):
    factor_of, own = 1.0, jax.random.fold_in(own_key, 6)
    for position, blocks in cuts:
        heights = jnp.exp(jax.random.uniform(jax.random.fold_in(own, position), (blocks,), jnp.float32, low / len(cuts), high / len(cuts)))
        factor_of = factor_of * jnp.repeat(heights, extent[position] // blocks).reshape([-1 if axis == position else 1 for axis in range(len(extent))])
    return factor_of


def bell_draw(key, shape, deviation, limit, shards=(), kind=jnp.bfloat16):
    result = jax.random.normal(key, shape, jnp.float32) * deviation
    if len(shards) > 0:
        result = steps_of(key, shape, shards, -0.22, 0.18) * result
    return jnp.clip(result, min=-limit, max=limit).astype(kind)


def setup_inputs(seed: int = 0) -> dict:
    key_of = jax.random.split(jax.random.key(seed), 5)
    object_field = bell_draw(key_of[0], (2, OBJ_R, OBJ_C), 1.0, 6.0, ((1, 8), (2, 16)), jnp.float32)
    probe_field = bell_draw(key_of[1], (2, PROBE, PROBE), 1.0, 6.0, (), jnp.float32)
    measured = jnp.clip(0.5 + 2.0 * jax.random.uniform(key_of[2], (POSITIONS, PROBE, PROBE), jnp.float32) ** steps_of(key_of[2], (POSITIONS, PROBE, PROBE), ((0, 128),), -0.2, 0.2), 0.5, 2.5)
    offsets = draw_offsets(jax.random.fold_in(key_of[4], 71), 0)
    return {"object_field": object_field, "probe_field": probe_field, "measured": measured, "offsets": offsets}


def reference(object_field, probe_field, measured, offsets):
    rim_width = PROBE // 2
    padded = jnp.pad(object_field, ((0, 0), (rim_width, rim_width), (rim_width, rim_width)))
    probe_c = lax.complex(probe_field[0], probe_field[1])

    def visit(carry, item):
        grad_pad, probe_sum = carry
        start, amplitude = item
        row_start = (start[0] + rim_width).astype(jnp.int32)
        col_start = (start[1] + rim_width).astype(jnp.int32)
        zero_index = jnp.int32(0)
        patch = lax.dynamic_slice(padded, (zero_index, row_start, col_start), (2, PROBE, PROBE))
        patch_c = lax.complex(patch[0], patch[1])
        wave = jnp.fft.fft2(probe_c * patch_c, norm='ortho')
        factor = 1.0 - amplitude / jnp.maximum(jnp.abs(wave), 1.0)
        back = jnp.fft.ifft2(wave * factor, norm='ortho')
        patch_grad = jnp.conj(probe_c) * back
        stacked = jnp.stack([jnp.real(patch_grad), jnp.imag(patch_grad)])
        current = lax.dynamic_slice(grad_pad, (zero_index, row_start, col_start), (2, PROBE, PROBE))
        grad_pad = lax.dynamic_update_slice(grad_pad, current + stacked, (zero_index, row_start, col_start))
        probe_sum = probe_sum + jnp.conj(patch_c) * back
        return ((grad_pad, probe_sum), None)
    init = (jnp.zeros_like(padded), jnp.zeros_like(probe_c))
    (grad_pad, probe_sum), _ = lax.scan(visit, init, (offsets, measured))
    object_grad = grad_pad[:, rim_width:rim_width + OBJ_R, rim_width:rim_width + OBJ_C]
    scale = 1.0 / jnp.sqrt(jnp.float32(POSITIONS))
    probe_grad = jnp.stack([jnp.real(probe_sum), jnp.imag(probe_sum)]) * scale
    return (object_grad, probe_grad.astype(object_field.dtype))
```

```python
import functools
import math

import jax
import jax.numpy as jnp
import numpy as np
from jax import lax
from jax.experimental import pallas as pl
from jax.experimental.pallas import tpu as pltpu
from jax.sharding import PartitionSpec as P

LANES = 128
RIM = 128
F32 = jnp.float32
BF16 = jnp.bfloat16
MESH = pl.DeviceIdType.MESH


def dft_tables(size):
    half = size // 2
    n = np.arange(half)[:, None]
    k = np.arange(half)[None, :]
    out = []
    for parity in range(2):
        phase = (n * (2 * k + parity)) % size
        table = np.exp(-2j * np.pi * phase / size) / math.sqrt(size)
        real = np.block([[table.real, table.imag], [-table.imag, table.real]])
        out += [real, real.T]
    stack = np.stack(out)
    high = stack.astype(np.float32).astype(BF16)
    low = (stack - high.astype(np.float64)).astype(np.float32).astype(BF16)
    return np.stack([high, low], axis=1)


def orderings(size):
    order = np.concatenate([np.arange(0, size, 2), np.arange(1, size, 2)])
    rows = np.zeros((size, size), np.float32)
    rows[np.arange(size), order] = 1.0
    return np.stack([rows, rows.T]).astype(BF16)


def split(value):
    high = value.astype(BF16)
    return high, (value - high.astype(F32)).astype(BF16)


def dot(a, b):
    return jnp.dot(a, b, preferred_element_type=F32)


def cat(parts, axis):
    return tuple(jnp.concatenate(p, axis=axis) for p in zip(*parts))


def one_position(chunk, row, col, meas, ext_ref, probe_ref, tab_ref, acc_ref, term_ref, rolled):
    size, half = 256, 128
    lane = lax.broadcasted_iota(jnp.int32, (chunk, LANES), 1)
    block = col // LANES
    shift = lax.rem(col, LANES)
    mask = lane >= shift

    def patch(start):
        rows = pl.ds(row + start, chunk)
        out = []
        for plane in range(2):
            b0 = ext_ref[plane, block, rows, :]
            b1 = ext_ref[plane, block + 1, rows, :]
            b2 = ext_ref[plane, block + 2, rows, :]
            out.append((jnp.where(mask, b0, b2), b1))
        return out

    sums, diffs = [], []
    for start in range(0, size, chunk):
        rows = pl.ds(start, chunk)
        (x0r, x1r), (x0i, x1i) = patch(start)
        pr = []
        for plane in range(2):
            r0 = pltpu.roll(probe_ref[plane, 0, rows, :], shift, 1)
            r1 = pltpu.roll(probe_ref[plane, 1, rows, :], shift, 1)
            p0 = jnp.where(mask, r0, r1)
            p1 = jnp.where(mask, r1, r0)
            rolled[plane, 0, rows, :] = p0
            rolled[plane, 1, rows, :] = p1
            pr.append((p0, p1))
        (p0r, p1r), (p0i, p1i) = pr
        e0r = p0r * x0r - p0i * x0i
        e0i = p0r * x0i + p0i * x0r
        e1r = p1r * x1r - p1i * x1i
        e1i = p1r * x1i + p1i * x1r
        sums.append(cat([split(e0r + e1r), split(e0i + e1i)], 1))
        diffs.append(cat([split(e0r - e1r), split(e0i - e1i)], 1))
    a, b = cat(sums, 0), cat(diffs, 0)

    def right(data, index):
        t = tab_ref[index, 0]
        return dot(data[0], t) + dot(data[1], t) + dot(data[0], tab_ref[index, 1])

    def left(index, data):
        t = tab_ref[index, 0]
        return dot(t, data[0]) + dot(t, data[1]) + dot(tab_ref[index, 1], data[0])

    yield
    ye = right(a, 0)
    yo = right(b, 2)
    yield
    s = [y[:half] + y[half:] for y in (ye, yo)]
    d = [y[:half] - y[half:] for y in (ye, yo)]
    a, b = [cat([cat([split(v[:, :LANES]) for v in w], 1), cat([split(v[:, LANES:]) for v in w], 1)], 0)
            for w in (s, d)]
    yield
    ze = left(1, a)
    zo = left(3, b)
    yield
    outs = []
    for z, first in ((ze, 0), (zo, half)):
        zr, zi = z[:half], z[half:]
        power = zr * zr + zi * zi
        factor = 1.0 - meas[pl.ds(first, half), :] * lax.rsqrt(jnp.maximum(power, 1.0))
        outs.append(cat([split(zr * factor), split(zi * factor)], 0))
    a, b = outs
    yield
    e = left(0, a)
    o = left(2, b)
    yield
    s, d = e + o, e - o
    a, b = [cat([cat([split(v[:half, cols]), split(v[half:, cols])], 1) for v in (s, d)], 0)
            for cols in (slice(0, LANES), slice(LANES, 2 * LANES))]
    yield
    e = right(a, 1)
    o = right(b, 3)
    yield
    back_shift = lax.rem(LANES - shift, LANES)
    keep = lane < LANES - shift
    for start in range(0, size, chunk):
        rows = pl.ds(start, chunk)
        ee, oo = e[start:start + chunk], o[start:start + chunk]
        b0, b1 = ee + oo, ee - oo
        b0r, b0i = b0[:, :LANES], b0[:, LANES:]
        b1r, b1i = b1[:, :LANES], b1[:, LANES:]
        p0r, p1r = rolled[0, 0, rows, :], rolled[0, 1, rows, :]
        p0i, p1i = rolled[1, 0, rows, :], rolled[1, 1, rows, :]
        grads = ((p0r * b0r + p0i * b0i, p1r * b1r + p1i * b1i),
                 (p0r * b0i - p0i * b0r, p1r * b1i - p1i * b1r))
        (x0r, x1r), (x0i, x1i) = patch(start)
        dst = pl.ds(row + start, chunk)
        for plane, (g0, g1) in enumerate(grads):
            acc_ref[plane, block, dst, :] += jnp.where(mask, g0, 0.0)
            acc_ref[plane, block + 1, dst, :] += g1
            acc_ref[plane, block + 2, dst, :] += jnp.where(mask, 0.0, g0)
        terms = ((x0r * b0r + x0i * b0i, x1r * b1r + x1i * b1i),
                 (x0r * b0i - x0i * b0r, x1r * b1i - x1i * b1r))
        for plane, (t0, t1) in enumerate(terms):
            r0 = pltpu.roll(t0, back_shift, 1)
            r1 = pltpu.roll(t1, back_shift, 1)
            term_ref[plane, 0, rows, :] += jnp.where(keep, r0, r1)
            term_ref[plane, 1, rows, :] += jnp.where(keep, r1, r0)


def compute_kernel(per_step, chunk, stagger, off_ref, ext_ref, probe_ref, meas_ref, tab_ref,
                   acc_ref, term_ref, rolled):
    step = pl.program_id(0)

    @pl.when(step == 0)
    def _():
        acc_ref[...] = jnp.zeros_like(acc_ref)
        term_ref[...] = jnp.zeros_like(term_ref)

    live = []
    for slot in range(per_step):
        pos = step * per_step + slot
        row = lax.rem(off_ref[pos, 0] + 128, 256)
        col = lax.rem(off_ref[pos, 1] + 128, 512)
        live.append(one_position(chunk, row, col, meas_ref.at[slot], ext_ref, probe_ref, tab_ref,
                                 acc_ref, term_ref, rolled.at[slot]))
    stages = 9
    for tick in range(stages + stagger * (per_step - 1)):
        for slot, gen in enumerate(live):
            if 0 <= tick - stagger * slot < stages:
                next(gen, None)


def compute(offsets, ext, probe, meas, tables, per_step=1, chunk=32, stagger=1):
    count = offsets.shape[0]
    whole = lambda a: pl.BlockSpec(a.shape, lambda i: (0,) * a.ndim)
    return pl.pallas_call(
        functools.partial(compute_kernel, per_step, chunk, stagger),
        grid=(count // per_step,),
        in_specs=[
            pl.BlockSpec(memory_space=pltpu.SMEM),
            whole(ext), whole(probe),
            pl.BlockSpec((per_step, 256, 256), lambda i: (i, 0, 0)),
            whole(tables),
        ],
        out_specs=[whole(ext), whole(probe)],
        out_shape=[jax.ShapeDtypeStruct(ext.shape, F32), jax.ShapeDtypeStruct(probe.shape, F32)],
        scratch_shapes=[pltpu.VMEM((per_step, 2, 2, 256, 128), F32)],
        compiler_params=pltpu.CompilerParams(vmem_limit_bytes=48 * 2**20),
        name="updates",
    )(offsets, ext, probe, meas, tables)


POS, TILE = "pos", "tile"
DIRECTIONS = tuple((dy, dx) for dy in (-1, 0, 1) for dx in (-1, 0, 1) if (dy, dx) != (0, 0))


def neighbour(dy, dx):
    p, t = lax.axis_index(POS), lax.axis_index(TILE)
    tp, tt = p + dx, t + dy
    inside = (tp >= 0) & (tp < lax.axis_size(POS)) & (tt >= 0) & (tt < lax.axis_size(TILE))
    return (tp, tt), inside


def region(dy, dx):
    rows = {-1: (0, RIM), 0: (RIM, 2 * RIM), 1: (3 * RIM, RIM)}[dy]
    blocks = {-1: (0, 1), 0: (1, 4), 1: (5, 1)}[dx]
    return rows, blocks


def greet(peers):
    barrier = pltpu.get_barrier_semaphore()
    for device, inside in peers:
        @pl.when(inside)
        def _():
            pl.semaphore_signal(barrier, inc=1, device_id=device, device_id_type=MESH)
    pl.semaphore_wait(barrier, sum(inside.astype(jnp.int32) for _, inside in peers))


def halo_kernel(obj_ref, meas_ref, perm_ref, ext_ref, out_ref, zeros, loaded, ordered, send_sem, recv_sem,
                fill_sem, own_sem, in_sem, out_sem):
    group = loaded.shape[0] // in_sem.shape[0]
    size = loaded.shape[1]
    loads = [pltpu.make_async_copy(meas_ref.at[pl.ds(g * group, group)], loaded.at[pl.ds(g * group, group)], in_sem.at[g])
             for g in range(in_sem.shape[0])]
    owns = [pltpu.make_async_copy(obj_ref.at[:, :, pl.ds(b * LANES, LANES)], ext_ref.at[:, b + 1, pl.ds(RIM, 2 * RIM), :],
                                  own_sem.at[b]) for b in range(4)]
    peers = [neighbour(*d) for d in DIRECTIONS]
    greet(peers)
    copies = []
    index = 0
    for (dy, dx), (device, inside) in zip(DIRECTIONS, peers):
        src_row, count = {-1: (0, RIM), 0: (0, 2 * RIM), 1: (RIM, RIM)}[dy]
        for b in {-1: (0,), 0: range(4), 1: (3,)}[dx]:
            (dst_row, _), (first, _) = region(-dy, -dx)
            dst_block = first + (b if dx == 0 else 0)
            copy = pltpu.make_async_remote_copy(
                src_ref=obj_ref.at[:, pl.ds(src_row, count), pl.ds(b * LANES, LANES)],
                dst_ref=ext_ref.at[:, dst_block, pl.ds(dst_row, count), :],
                send_sem=send_sem.at[index], recv_sem=recv_sem.at[index],
                device_id=device, device_id_type=MESH)
            _, from_inside = neighbour(-dy, -dx)
            fill = pltpu.make_async_copy(zeros.at[:, pl.ds(0, count), :],
                                         ext_ref.at[:, dst_block, pl.ds(dst_row, count), :], fill_sem.at[index])
            copies.append((copy, inside, from_inside, fill))
            index += 1

            @pl.when(inside)
            def _():
                copy.start()
    for load in loads:
        load.start()
    for own in owns:
        own.start()
    zeros[...] = jnp.zeros_like(zeros)
    for copy, inside, from_inside, fill in copies:
        @pl.when(jnp.logical_not(from_inside))
        def _():
            fill.start()
    perm_rows, perm_cols = perm_ref[0], perm_ref[1]
    stores = []
    for g in range(in_sem.shape[0]):
        loads[g].wait()

        def order(i, carry):
            at = g * group + 2 * i
            parts = [split(loaded[at + j]) for j in range(2)]
            done = None
            for k in range(2):
                rows = jnp.concatenate([parts[0][k], parts[1][k]], axis=0)
                moved = dot(rows, perm_cols).astype(BF16)
                moved = jnp.concatenate([moved[:size], moved[size:]], axis=1)
                moved = dot(perm_rows, moved)
                done = moved if done is None else done + moved
            ordered[at] = done[:, :size]
            ordered[at + 1] = done[:, size:]
            return carry

        lax.fori_loop(0, group // 2, order, 0)
        store = pltpu.make_async_copy(ordered.at[pl.ds(g * group, group)], out_ref.at[pl.ds(g * group, group)], out_sem.at[g])
        store.start()
        stores.append(store)
    for store in stores:
        store.wait()
    for own in owns:
        own.wait()
    for copy, inside, from_inside, fill in copies:
        @pl.when(inside)
        def _():
            copy.wait_send()

        @pl.when(from_inside)
        def _():
            copy.wait_recv()

        @pl.when(jnp.logical_not(from_inside))
        def _():
            fill.wait()


def exchange(object_field, measured, perms):
    count, size = measured.shape[0], measured.shape[1]
    groups = 4
    return pl.pallas_call(
        halo_kernel,
        in_specs=[pl.BlockSpec(memory_space=pl.ANY), pl.BlockSpec(memory_space=pl.ANY), pl.BlockSpec(memory_space=pltpu.VMEM)],
        out_specs=[pl.BlockSpec(memory_space=pl.ANY)] * 2,
        out_shape=[jax.ShapeDtypeStruct((2, 6, 4 * RIM, LANES), F32), jax.ShapeDtypeStruct(measured.shape, F32)],
        scratch_shapes=[
            pltpu.VMEM((2, 2 * RIM, LANES), F32),
            pltpu.VMEM(measured.shape, F32),
            pltpu.VMEM(measured.shape, F32),
            pltpu.SemaphoreType.DMA((14,)), pltpu.SemaphoreType.DMA((14,)), pltpu.SemaphoreType.DMA((14,)),
            pltpu.SemaphoreType.DMA((4,)), pltpu.SemaphoreType.DMA((groups,)), pltpu.SemaphoreType.DMA((groups,)),
        ],
        compiler_params=pltpu.CompilerParams(collective_id=0, has_side_effects=True, vmem_limit_bytes=40 * 2**20),
        name="halo",
    )(object_field, measured, perms)


def gather_kernel(acc_ref, term_ref, obj_ref, probe_ref, own, total, result, *rest):
    (recv_v, recv_h, recv_d, part1, part2, part3,
     load_sem, send_sem, recv_sem, s1, r1, s2, r2, s3, r3, s4, r4, s5, r5, s6, r6, out_sem, pout_sem) = rest
    p, t = lax.axis_index(POS), lax.axis_index(TILE)
    x, z = p // 4, lax.rem(p, 4)
    y, core = t // 2, lax.rem(t, 2)
    yz = y * 4 + z
    yes = p >= 0
    partner = (p, t + 1 - 2 * core)
    x_peers = [(lax.rem(x + k, 4) * 4 + z, t) for k in range(1, 4)]
    x_ids = [lax.rem(x + k, 4) for k in range(1, 4)]
    yz_ids = [lax.rem(yz + k, 16) for k in range(1, 16)]
    yz_peers = [(x * 4 + lax.rem(i, 4), (i // 4) * 2 + core) for i in yz_ids]
    around = [neighbour(*d) for d in DIRECTIONS]

    load_total = pltpu.make_async_copy(term_ref, total, load_sem.at[0])
    load_own = pltpu.make_async_copy(acc_ref.at[:, pl.ds(1, 4), pl.ds(RIM, 2 * RIM), :], own, load_sem.at[1])
    load_total.start()
    load_own.start()
    greet(around + [(partner, yes)] + [(d, yes) for d in x_peers] + [(d, yes) for d in yz_peers])

    def remote(src, dst, send, recv, device):
        return pltpu.make_async_remote_copy(src_ref=src, dst_ref=dst, send_sem=send, recv_sem=recv,
                                            device_id=device, device_id_type=MESH)

    load_total.wait()
    half = 512
    mine = pl.multiple_of(core * half, half)
    other = pl.multiple_of((1 - core) * half, half)
    first = remote(total.at[pl.ds(other, half)], part1, s1, r1, partner)
    first.start()
    copies = []
    for index, ((dy, dx), (device, inside)) in enumerate(zip(DIRECTIONS, around)):
        (row, rows), (block, blocks) = region(dy, dx)
        slot = {-1: 0, 1: 1}
        if dx == 0:
            dst = recv_v.at[slot[dy]]
        elif dy == 0:
            dst = recv_h.at[slot[dx]]
        else:
            dst = recv_d.at[slot[dy] * 2 + slot[dx]]
        copy = remote(acc_ref.at[:, pl.ds(block, blocks), pl.ds(row, rows), :], dst, send_sem.at[index], recv_sem.at[index], device)
        _, from_inside = neighbour(-dy, -dx)
        copies.append((copy, inside, from_inside, dst, dy, dx))

        @pl.when(inside)
        def _():
            copy.start()
    first.wait()
    total[pl.ds(mine, half)] = total[pl.ds(mine, half)] + part1[...]
    quarter = half // 4
    seconds = [remote(total.at[pl.ds(pl.multiple_of(mine + i * quarter, quarter), quarter)], part2.at[k], s2.at[k], r2.at[k], d)
               for k, (i, d) in enumerate(zip(x_ids, x_peers))]
    for c in seconds:
        c.start()
    load_own.wait()
    for c in seconds:
        c.wait()
    at2 = pl.multiple_of(mine + x * quarter, quarter)
    total[pl.ds(at2, quarter)] = total[pl.ds(at2, quarter)] + part2[0] + part2[1] + part2[2]
    piece = quarter // 16
    thirds = [remote(total.at[pl.ds(pl.multiple_of(at2 + i * piece, piece), piece)], part3.at[k], s3.at[k], r3.at[k], d)
              for k, (i, d) in enumerate(zip(yz_ids, yz_peers))]
    for c in thirds:
        c.start()
    for c in thirds:
        c.wait()
    at3 = pl.multiple_of(at2 + yz * piece, piece)
    value = total[pl.ds(at3, piece)]
    for k in range(15):
        value = value + part3[k]
    result[pl.ds(at3, piece)] = value * (1.0 / math.sqrt(2048))
    here = result.at[pl.ds(at3, piece)]
    fourths = [remote(here, here, s4.at[k], r4.at[k], d) for k, d in enumerate(yz_peers)]
    for c in fourths:
        c.start()
    outs = []
    for copy, inside, from_inside, dst, dy, dx in copies:
        to_row, to_rows = {-1: (RIM, RIM), 0: (0, 2 * RIM), 1: (0, RIM)}[dy]
        to_block, blocks = {-1: (3, 1), 0: (0, 4), 1: (0, 1)}[dx]

        @pl.when(from_inside)
        def _():
            copy.wait_recv()
            def add(i, carry):
                b = i // 2
                rows = pl.ds(to_row, to_rows)
                own[lax.rem(i, 2), to_block + b, rows, :] = own[lax.rem(i, 2), to_block + b, rows, :] + dst[lax.rem(i, 2), b]
                return carry
            lax.fori_loop(0, 2 * blocks, add, 0)

        @pl.when(inside)
        def _():
            copy.wait_send()
    for b in range(4):
        out = pltpu.make_async_copy(own.at[:, b], obj_ref.at[:, :, pl.ds(b * LANES, LANES)], out_sem.at[b])
        out.start()
        outs.append(out)
    for c in fourths:
        c.wait()
    here2 = result.at[pl.ds(at2, quarter)]
    fifths = [remote(here2, here2, s5.at[k], r5.at[k], d) for k, d in enumerate(x_peers)]
    for c in fifths:
        c.start()
    for c in fifths:
        c.wait()
    here1 = result.at[pl.ds(mine, half)]
    last = remote(here1, here1, s6, r6, partner)
    last.start()
    last.wait()
    for i in range(4):
        out = pltpu.make_async_copy(result.at[pl.ds(i * 256, 256)], probe_ref.at[i // 2, :, pl.ds((i % 2) * LANES, LANES)], pout_sem.at[i])
        out.start()
        outs.append(out)
    for out in outs:
        out.wait()


def collect(acc, term):
    dma = pltpu.SemaphoreType.DMA
    return pl.pallas_call(
        gather_kernel,
        in_specs=[pl.BlockSpec(memory_space=pl.ANY)] * 2,
        out_specs=[pl.BlockSpec(memory_space=pl.ANY)] * 2,
        out_shape=[jax.ShapeDtypeStruct((2, 256, 512), F32), jax.ShapeDtypeStruct((2, 256, 256), F32)],
        scratch_shapes=[
            pltpu.VMEM((2, 4, 2 * RIM, LANES), F32),
            pltpu.VMEM((1024, LANES), F32),
            pltpu.VMEM((1024, LANES), F32),
            pltpu.VMEM((2, 2, 4, RIM, LANES), F32),
            pltpu.VMEM((2, 2, 1, 2 * RIM, LANES), F32),
            pltpu.VMEM((4, 2, 1, RIM, LANES), F32),
            pltpu.VMEM((512, LANES), F32),
            pltpu.VMEM((3, 128, LANES), F32),
            pltpu.VMEM((15, 8, LANES), F32),
            dma((2,)), dma((8,)), dma((8,)), dma, dma, dma((3,)), dma((3,)), dma((15,)), dma((15,)),
            dma((15,)), dma((15,)), dma((3,)), dma((3,)), dma, dma, dma((4,)), dma((4,)),
        ],
        compiler_params=pltpu.CompilerParams(collective_id=1, has_side_effects=True, vmem_limit_bytes=40 * 2**20),
        name="collect",
    )(acc, term.reshape(1024, LANES))


def on_device(object_field, probe_field, measured, offsets):
    ext, ordered = exchange(object_field, measured, jnp.asarray(orderings(256)))
    probe = jnp.stack([probe_field[:, :, :LANES], probe_field[:, :, LANES:]], axis=1)
    acc, term = compute(offsets, ext, probe, ordered, jnp.asarray(dft_tables(256)), per_step=2)
    return collect(acc, term)


def solution(mesh):
    placed = (P(None, "tile", "pos"), P(), P(("pos", "tile"), None, None), P(("pos", "tile"), None))
    return jax.shard_map(
        on_device,
        mesh=mesh,
        in_specs=placed,
        out_specs=(P(None, "tile", "pos"), P()),
        check_vma=False,
    )
```

```python
import functools
import math

import jax
import jax.numpy as jnp
import numpy as np
from jax import lax
from jax.experimental import pallas as pl
from jax.experimental.pallas import tpu as pltpu
from jax.sharding import PartitionSpec as P

LANES = 128
RIM = 128
F32 = jnp.float32
BF16 = jnp.bfloat16
MESH = pl.DeviceIdType.MESH


def dft_tables(size):
    half = size // 2
    n = np.arange(half)[:, None]
    k = np.arange(half)[None, :]
    out = []
    for parity in range(2):
        phase = (n * (2 * k + parity)) % size
        table = np.exp(-2j * np.pi * phase / size) / math.sqrt(size)
        real = np.block([[table.real, table.imag], [-table.imag, table.real]])
        out += [real, real.T]
    stack = np.stack(out)
    high = stack.astype(np.float32).astype(BF16)
    low = (stack - high.astype(np.float64)).astype(np.float32).astype(BF16)
    return np.stack([high, low], axis=1)


def split(value):
    high = value.astype(BF16)
    return high, (value - high.astype(F32)).astype(BF16)


def dot(a, b):
    return jnp.dot(a, b, preferred_element_type=F32)


def cat(parts, axis):
    return tuple(jnp.concatenate(p, axis=axis) for p in zip(*parts))


def one_position(chunk, row, col, meas, ext_ref, probe_ref, tab_ref, acc_ref, term_ref, rolled):
    size, half = 256, 128
    lane = lax.broadcasted_iota(jnp.int32, (chunk, LANES), 1)
    block = col // LANES
    shift = lax.rem(col, LANES)
    mask = lane >= shift

    def patch(start):
        rows = pl.ds(row + start, chunk)
        out = []
        for plane in range(2):
            b0 = ext_ref[plane, block, rows, :]
            b1 = ext_ref[plane, block + 1, rows, :]
            b2 = ext_ref[plane, block + 2, rows, :]
            out.append((jnp.where(mask, b0, b2), b1))
        return out

    sums, diffs = [], []
    for start in range(0, size, chunk):
        rows = pl.ds(start, chunk)
        (x0r, x1r), (x0i, x1i) = patch(start)
        pr = []
        for plane in range(2):
            r0 = pltpu.roll(probe_ref[plane, 0, rows, :], shift, 1)
            r1 = pltpu.roll(probe_ref[plane, 1, rows, :], shift, 1)
            p0 = jnp.where(mask, r0, r1)
            p1 = jnp.where(mask, r1, r0)
            rolled[plane, 0, rows, :] = p0
            rolled[plane, 1, rows, :] = p1
            pr.append((p0, p1))
        (p0r, p1r), (p0i, p1i) = pr
        e0r = p0r * x0r - p0i * x0i
        e0i = p0r * x0i + p0i * x0r
        e1r = p1r * x1r - p1i * x1i
        e1i = p1r * x1i + p1i * x1r
        sums.append(cat([split(e0r + e1r), split(e0i + e1i)], 1))
        diffs.append(cat([split(e0r - e1r), split(e0i - e1i)], 1))
    a, b = cat(sums, 0), cat(diffs, 0)

    def right(data, index):
        t = tab_ref[index, 0]
        return dot(data[0], t) + dot(data[1], t) + dot(data[0], tab_ref[index, 1])

    def left(index, data):
        t = tab_ref[index, 0]
        return dot(t, data[0]) + dot(t, data[1]) + dot(tab_ref[index, 1], data[0])

    yield
    ye = right(a, 0)
    yo = right(b, 2)
    yield
    s = [y[:half] + y[half:] for y in (ye, yo)]
    d = [y[:half] - y[half:] for y in (ye, yo)]
    a, b = [cat([cat([split(v[:, :LANES]) for v in w], 1), cat([split(v[:, LANES:]) for v in w], 1)], 0)
            for w in (s, d)]
    yield
    ze = left(1, a)
    zo = left(3, b)
    yield
    outs = []
    for z, first in ((ze, 0), (zo, half)):
        zr, zi = z[:half], z[half:]
        power = zr * zr + zi * zi
        factor = 1.0 - meas[pl.ds(first, half), :] * lax.rsqrt(jnp.maximum(power, 1.0))
        outs.append(cat([split(zr * factor), split(zi * factor)], 0))
    a, b = outs
    yield
    e = left(0, a)
    o = left(2, b)
    yield
    s, d = e + o, e - o
    a, b = [cat([cat([split(v[:half, cols]), split(v[half:, cols])], 1) for v in (s, d)], 0)
            for cols in (slice(0, LANES), slice(LANES, 2 * LANES))]
    yield
    e = right(a, 1)
    o = right(b, 3)
    yield
    back_shift = lax.rem(LANES - shift, LANES)
    keep = lane < LANES - shift
    for start in range(0, size, chunk):
        rows = pl.ds(start, chunk)
        ee, oo = e[start:start + chunk], o[start:start + chunk]
        b0, b1 = ee + oo, ee - oo
        b0r, b0i = b0[:, :LANES], b0[:, LANES:]
        b1r, b1i = b1[:, :LANES], b1[:, LANES:]
        p0r, p1r = rolled[0, 0, rows, :], rolled[0, 1, rows, :]
        p0i, p1i = rolled[1, 0, rows, :], rolled[1, 1, rows, :]
        grads = ((p0r * b0r + p0i * b0i, p1r * b1r + p1i * b1i),
                 (p0r * b0i - p0i * b0r, p1r * b1i - p1i * b1r))
        (x0r, x1r), (x0i, x1i) = patch(start)
        dst = pl.ds(row + start, chunk)
        for plane, (g0, g1) in enumerate(grads):
            acc_ref[plane, block, dst, :] += jnp.where(mask, g0, 0.0)
            acc_ref[plane, block + 1, dst, :] += g1
            acc_ref[plane, block + 2, dst, :] += jnp.where(mask, 0.0, g0)
        terms = ((x0r * b0r + x0i * b0i, x1r * b1r + x1i * b1i),
                 (x0r * b0i - x0i * b0r, x1r * b1i - x1i * b1r))
        for plane, (t0, t1) in enumerate(terms):
            r0 = pltpu.roll(t0, back_shift, 1)
            r1 = pltpu.roll(t1, back_shift, 1)
            term_ref[plane, 0, rows, :] += jnp.where(keep, r0, r1)
            term_ref[plane, 1, rows, :] += jnp.where(keep, r1, r0)


def compute_kernel(per_step, chunk, off_ref, ext_ref, probe_ref, meas_ref, tab_ref, acc_ref, term_ref, rolled):
    acc_ref[...] = jnp.zeros_like(acc_ref)
    term_ref[...] = jnp.zeros_like(term_ref)
    stages = 9

    def step(index, carry):
        live = []
        for slot in range(per_step):
            pos = index * per_step + slot
            row = lax.rem(off_ref[0, pos] + 128, 256)
            col = lax.rem(off_ref[1, pos] + 128, 512)
            live.append(one_position(chunk, row, col, meas_ref.at[pos], ext_ref, probe_ref, tab_ref,
                                     acc_ref, term_ref, rolled.at[slot]))
        for tick in range(stages + per_step - 1):
            for slot, gen in enumerate(live):
                if 0 <= tick - slot < stages:
                    next(gen, None)
        return carry

    lax.fori_loop(0, meas_ref.shape[0] // per_step, step, 0)


def compute(offsets, ext, probe, meas, tables, per_step=2, chunk=32):
    vmem = pl.BlockSpec(memory_space=pltpu.VMEM)
    return pl.pallas_call(
        functools.partial(compute_kernel, per_step, chunk),
        in_specs=[pl.BlockSpec(memory_space=pltpu.SMEM)] + [vmem] * 4,
        out_specs=[vmem] * 2,
        out_shape=[jax.ShapeDtypeStruct(ext.shape, F32), jax.ShapeDtypeStruct(probe.shape, F32)],
        scratch_shapes=[pltpu.VMEM((per_step, 2, 2, 256, 128), F32)],
        compiler_params=pltpu.CompilerParams(vmem_limit_bytes=32 * 2**20),
        name="updates",
    )(offsets, ext, probe, meas, tables)


POS, TILE = "pos", "tile"


def neighbour(dy, dx):
    p, t = lax.axis_index(POS), lax.axis_index(TILE)
    tp, tt = p + dx, t + dy
    inside = (tp >= 0) & (tp < lax.axis_size(POS)) & (tt >= 0) & (tt < lax.axis_size(TILE))
    return (tp, tt), inside


def greet(peers):
    barrier = pltpu.get_barrier_semaphore()
    for device, inside in peers:
        @pl.when(inside)
        def _():
            pl.semaphore_signal(barrier, inc=1, device_id=device, device_id_type=MESH)
    pl.semaphore_wait(barrier, sum(inside.astype(jnp.int32) for _, inside in peers))


def chip_side():
    core = lax.rem(lax.axis_index(TILE), 2)
    inner = 1 - 2 * core
    return core, inner, (lax.axis_index(POS), lax.axis_index(TILE) + inner)


def remote(src, dst, send, recv, device):
    return pltpu.make_async_remote_copy(src_ref=src, dst_ref=dst, send_sem=send, recv_sem=recv,
                                        device_id=device, device_id_type=MESH)


def when_each(condition, *calls):
    @pl.when(condition)
    def _():
        for call in calls:
            call()


def order_table(rows_first, size):
    out = lax.broadcasted_iota(jnp.int32, (size, size), 0 if rows_first else 1)
    src = lax.broadcasted_iota(jnp.int32, (size, size), 1 if rows_first else 0)
    half = size // 2
    wanted = jnp.where(out < half, 2 * out, 2 * out - size + 1)
    return jnp.where(src == wanted, 1.0, 0.0).astype(BF16)


def halo_kernel(obj_ref, meas_ref, prb_ref, ext_ref, out_ref, probe_ref, zeros, loaded, ordered, send_sem, recv_sem,
                fill_sem, own_sem, in_sem, out_sem, relay_send, relay_recv, probe_sem):
    group = loaded.shape[0] // in_sem.shape[0]
    size = loaded.shape[1]
    core, inner, partner = chip_side()
    p, t = lax.axis_index(POS), lax.axis_index(TILE)
    loads = [pltpu.make_async_copy(meas_ref.at[pl.ds(g * group, group)], loaded.at[pl.ds(g * group, group)], in_sem.at[g])
             for g in range(in_sem.shape[0])]
    locals_ = [pltpu.make_async_copy(obj_ref.at[:, :, pl.ds(b * LANES, LANES)], ext_ref.at[:, b + 1, pl.ds(RIM, 2 * RIM), :],
                                     own_sem.at[b]) for b in range(4)]
    locals_ += [pltpu.make_async_copy(prb_ref.at[:, :, pl.ds(b * LANES, LANES)], probe_ref.at[:, b], probe_sem.at[b])
                for b in range(2)]
    sides = [neighbour(0, -1), neighbour(0, 1)]
    outer, outer_in = neighbour(-inner, 0)
    corners = [neighbour(-inner, -1), neighbour(-inner, 1)]
    for load in loads:
        load.start()
    greet(sides + corners + [(outer, outer_in), (partner, p >= 0)])
    inner_row = pl.multiple_of((1 - core) * RIM, RIM)
    outer_row = pl.multiple_of(core * RIM, RIM)
    inner_halo = pl.multiple_of((1 - core) * 3 * RIM, RIM)
    outer_halo = pl.multiple_of(core * 3 * RIM, RIM)
    pairs = []

    def add(src_row, count, block, dst_block, dst_row, device, there, source_there, fill_row):
        index = len(pairs)
        copy = remote(obj_ref.at[:, pl.ds(src_row, count), pl.ds(block * LANES, LANES)],
                      ext_ref.at[:, dst_block, pl.ds(dst_row, count), :], send_sem.at[index], recv_sem.at[index], device)
        fill = pltpu.make_async_copy(zeros.at[:, pl.ds(0, count), :], ext_ref.at[:, dst_block, pl.ds(fill_row, count), :],
                                     fill_sem.at[index])
        pairs.append((copy, there, source_there, fill))
        when_each(there, copy.start)

    add(0, 2 * RIM, 0, 5, RIM, sides[0][0], sides[0][1], sides[1][1], RIM)
    add(0, 2 * RIM, 3, 0, RIM, sides[1][0], sides[1][1], sides[0][1], RIM)
    there_row = pl.multiple_of((1 - core) * 3 * RIM, RIM)
    for b in range(4):
        add(outer_row, RIM, b, b + 1, there_row, outer, outer_in, outer_in, outer_halo)
    add(outer_row, RIM, 0, 5, there_row, corners[0][0], corners[0][1], corners[1][1], outer_halo)
    add(outer_row, RIM, 3, 0, there_row, corners[1][0], corners[1][1], corners[0][1], outer_halo)
    partner_halo = pl.multiple_of(core * 3 * RIM, RIM)
    inside = [remote(obj_ref.at[:, pl.ds(inner_row, RIM), pl.ds(b * LANES, LANES)],
                     ext_ref.at[:, b + 1, pl.ds(partner_halo, RIM), :], relay_send.at[b], relay_recv.at[b], partner)
              for b in range(4)]
    for copy in inside:
        copy.start()
    for copy in locals_:
        copy.start()
    zeros[...] = jnp.zeros_like(zeros)
    for copy, there, source_there, fill in pairs:
        when_each(jnp.logical_not(source_there), fill.start)
    perm_rows, perm_cols = order_table(True, size), order_table(False, size)
    stores = []

    def relay():
        made = []
        inner_own = pl.multiple_of((2 - core) * RIM, RIM)
        for k, block in enumerate((5, 0)):
            copy, there, source_there, fill = pairs[k]
            when_each(source_there, copy.wait_recv)
            when_each(jnp.logical_not(source_there), fill.wait)
            here = ext_ref.at[:, block, pl.ds(inner_own, RIM), :]
            there_ref = ext_ref.at[:, block, pl.ds(partner_halo, RIM), :]
            made.append(remote(here, there_ref, relay_send.at[4 + k], relay_recv.at[4 + k], partner))
            made[-1].start()
        return made

    for g in range(in_sem.shape[0]):
        loads[g].wait()

        def order(i, carry):
            at = g * group + 2 * i
            parts = [split(loaded[at + j]) for j in range(2)]
            done = None
            for k in range(2):
                rows = jnp.concatenate([parts[0][k], parts[1][k]], axis=0)
                moved = dot(rows, perm_cols).astype(BF16)
                moved = jnp.concatenate([moved[:size], moved[size:]], axis=1)
                moved = dot(perm_rows, moved)
                done = moved if done is None else done + moved
            ordered[at] = done[:, :size]
            ordered[at + 1] = done[:, size:]
            return carry

        lax.fori_loop(0, group // 2, order, 0)
        store = pltpu.make_async_copy(ordered.at[pl.ds(g * group, group)], out_ref.at[pl.ds(g * group, group)], out_sem.at[g])
        store.start()
        stores.append(store)
    inside += relay()
    for copy in stores + locals_:
        copy.wait()
    for index, (copy, there, source_there, fill) in enumerate(pairs):
        when_each(there, copy.wait_send)
        if index >= 2:
            when_each(source_there, copy.wait_recv)
            when_each(jnp.logical_not(source_there), fill.wait)
    for copy in inside:
        copy.wait()


def exchange(object_field, measured, probe_field):
    groups = 4
    dma = pltpu.SemaphoreType.DMA
    anywhere = pl.BlockSpec(memory_space=pl.ANY)
    return pl.pallas_call(
        halo_kernel,
        in_specs=[pl.BlockSpec(memory_space=pltpu.HBM)] * 3,
        out_specs=[anywhere] * 3,
        out_shape=[jax.ShapeDtypeStruct((2, 6, 4 * RIM, LANES), F32), jax.ShapeDtypeStruct(measured.shape, F32),
                   jax.ShapeDtypeStruct((2, 2, 2 * RIM, LANES), F32)],
        scratch_shapes=[
            pltpu.VMEM((2, 2 * RIM, LANES), F32),
            pltpu.VMEM(measured.shape, F32),
            pltpu.VMEM(measured.shape, F32),
            dma((8,)), dma((8,)), dma((8,)),
            dma((4,)), dma((groups,)), dma((groups,)), dma((6,)), dma((6,)), dma((2,)),
        ],
        compiler_params=pltpu.CompilerParams(collective_id=0, has_side_effects=True, vmem_limit_bytes=16 * 2**20),
        name="halo",
    )(object_field, measured, probe_field)


LATE = 1
OUT_SPACE = pl.ANY


def gather_kernel(acc_ref, term_ref, obj_ref, probe_ref, own, total, result, *rest):
    (recv_v, recv_in, recv_c, recv_h, recv_d, side, part1, part2, part3,
     load_sem, send_sem, recv_sem, s1, r1, s2, r2, s3, r3, s4, r4, s5, r5, s6, r6, out_sem, pout_sem) = rest
    p, t = lax.axis_index(POS), lax.axis_index(TILE)
    x, z = p // 4, lax.rem(p, 4)
    y = t // 2
    core, inner, partner = chip_side()
    yz = y * 4 + z
    yes = p >= 0
    x_peers = [(lax.rem(x + k, 4) * 4 + z, t) for k in range(1, 4)]
    x_ids = [lax.rem(x + k, 4) for k in range(1, 4)]
    yz_ids = [lax.rem(yz + k, 16) for k in range(1, 16)]
    yz_peers = [(x * 4 + lax.rem(i, 4), (i // 4) * 2 + core) for i in yz_ids]
    sides = [neighbour(0, -1), neighbour(0, 1)]
    outer, outer_in = neighbour(-inner, 0)
    corners = [neighbour(-inner, -1), neighbour(-inner, 1)]

    load_total = pltpu.make_async_copy(term_ref, total, load_sem.at[0])
    load_own = pltpu.make_async_copy(acc_ref.at[:, pl.ds(1, 4), pl.ds(RIM, 2 * RIM), :], own, load_sem.at[1])
    load_sides = [pltpu.make_async_copy(acc_ref.at[:, b, pl.ds(RIM, 2 * RIM), :], side.at[k], load_sem.at[2 + k])
                  for k, b in enumerate((0, 5))]
    load_total.start()
    for load in load_sides:
        load.start()
    load_own.start()
    greet([(partner, yes), (outer, outer_in)] + sides + corners + [(d, yes) for d in x_peers] + [(d, yes) for d in yz_peers])
    load_total.wait()
    half = 512
    mine = pl.multiple_of(core * half, half)
    other = pl.multiple_of((1 - core) * half, half)
    first = remote(total.at[pl.ds(other, half)], part1, s1, r1, partner)
    first.start()
    inner_halo = pl.multiple_of((1 - core) * 3 * RIM, RIM)
    outer_halo = pl.multiple_of(core * 3 * RIM, RIM)
    count = 0

    def link(src, dst, device):
        nonlocal count
        copy = remote(src, dst, send_sem.at[count], recv_sem.at[count], device)
        count += 1
        return copy

    inner_corners = [link(acc_ref.at[:, b, pl.ds(inner_halo, RIM), :], recv_c.at[k], partner) for k, b in enumerate((0, 5))]
    for copy in inner_corners:
        copy.start()
    inner_main = link(acc_ref.at[:, pl.ds(1, 4), pl.ds(inner_halo, RIM), :], recv_in, partner)
    outer_main = link(acc_ref.at[:, pl.ds(1, 4), pl.ds(outer_halo, RIM), :], recv_v, outer)
    diagonal = [link(acc_ref.at[:, b, pl.ds(outer_halo, RIM), :], recv_d.at[k], corners[k][0]) for k, b in enumerate((0, 5))]
    across = [link(side.at[k], recv_h.at[k], sides[k][0]) for k in range(2)]
    when_each(outer_in, outer_main.start)
    for k in range(2):
        when_each(corners[k][1], diagonal[k].start)
    inner_main.start()
    first.wait()
    total[pl.ds(mine, half)] = total[pl.ds(mine, half)] + part1[...]
    quarter = half // 4
    seconds = [remote(total.at[pl.ds(pl.multiple_of(mine + i * quarter, quarter), quarter)], part2.at[k], s2.at[k], r2.at[k], d)
               for k, (i, d) in enumerate(zip(x_ids, x_peers))]
    for c in seconds:
        c.start()
    near = pl.multiple_of((1 - core) * RIM, RIM)
    for k in range(2):
        inner_corners[k].wait()
        load_sides[k].wait()
        side[k, :, pl.ds(near, RIM), :] = side[k, :, pl.ds(near, RIM), :] + recv_c[k]
        if not LATE:
            when_each(sides[k][1], across[k].start)
    at2 = pl.multiple_of(mine + x * quarter, quarter)
    for c in seconds:
        c.wait()
    total[pl.ds(at2, quarter)] = total[pl.ds(at2, quarter)] + part2[0] + part2[1] + part2[2]
    piece = quarter // 16
    thirds = [remote(total.at[pl.ds(pl.multiple_of(at2 + i * piece, piece), piece)], part3.at[k], s3.at[k], r3.at[k], d)
              for k, (i, d) in enumerate(zip(yz_ids, yz_peers))]
    for c in thirds:
        c.start()
    if LATE == 1:
        for k in range(2):
            when_each(sides[k][1], across[k].start)
    load_own.wait()
    far = pl.multiple_of(core * RIM, RIM)
    inner_main.wait()

    def add_rows(src, at):
        def body(i, carry):
            plane, b = i // 4, lax.rem(i, 4)
            own[plane, b, pl.ds(at, RIM), :] = own[plane, b, pl.ds(at, RIM), :] + src[plane, b]
            return carry
        lax.fori_loop(0, 8, body, 0)

    add_rows(recv_in, near)
    for c in thirds:
        c.wait()
    at3 = pl.multiple_of(at2 + yz * piece, piece)
    value = total[pl.ds(at3, piece)]
    for k in range(15):
        value = value + part3[k]
    result[pl.ds(at3, piece)] = value * (1.0 / math.sqrt(2048))
    here = result.at[pl.ds(at3, piece)]
    fourths = [remote(here, here, s4.at[k], r4.at[k], d) for k, d in enumerate(yz_peers)]
    for c in fourths:
        c.start()
    if LATE == 2:
        for k in range(2):
            when_each(sides[k][1], across[k].start)

    @pl.when(outer_in)
    def _():
        outer_main.wait()
        add_rows(recv_v, far)

    outs = [pltpu.make_async_copy(own.at[:, b], obj_ref.at[:, :, pl.ds(b * LANES, LANES)], out_sem.at[b]) for b in range(4)]
    for b in (1, 2):
        outs[b].start()
    for c in fourths:
        c.wait()
    here2 = result.at[pl.ds(at2, quarter)]
    fifths = [remote(here2, here2, s5.at[k], r5.at[k], d) for k, d in enumerate(x_peers)]
    for c in fifths:
        c.start()
    for k in range(2):
        block = 3 - 3 * k
        source, diagonal_source = sides[1 - k][1], corners[1 - k][1]

        @pl.when(source)
        def _():
            across[k].wait_recv()
            own[:, block] = own[:, block] + recv_h[k]

        @pl.when(diagonal_source)
        def _():
            diagonal[k].wait_recv()
            own[:, block, pl.ds(far, RIM), :] = own[:, block, pl.ds(far, RIM), :] + recv_d[k]

        outs[block].start()
    for c in fifths:
        c.wait()
    here1 = result.at[pl.ds(mine, half)]
    last = remote(here1, here1, s6, r6, partner)
    last.start()
    for k in range(2):
        when_each(sides[k][1], across[k].wait_send)
        when_each(corners[k][1], diagonal[k].wait_send)
    last.wait()
    for i in range(4):
        out = pltpu.make_async_copy(result.at[pl.ds(i * 256, 256)], probe_ref.at[i // 2, :, pl.ds((i % 2) * LANES, LANES)], pout_sem.at[i])
        out.start()
        outs.append(out)
    for out in outs:
        out.wait()


def collect(acc, term):
    dma = pltpu.SemaphoreType.DMA
    vmem = lambda *shape: pltpu.VMEM(shape, F32)
    return pl.pallas_call(
        gather_kernel,
        in_specs=[pl.BlockSpec(memory_space=pl.ANY)] * 2,
        out_specs=[pl.BlockSpec(memory_space=OUT_SPACE)] * 2,
        out_shape=[jax.ShapeDtypeStruct((2, 256, 512), F32), jax.ShapeDtypeStruct((2, 256, 256), F32)],
        scratch_shapes=[
            vmem(2, 4, 2 * RIM, LANES), vmem(1024, LANES), vmem(1024, LANES),
            vmem(2, 4, RIM, LANES), vmem(2, 4, RIM, LANES), vmem(2, 2, RIM, LANES), vmem(2, 2, 2 * RIM, LANES),
            vmem(2, 2, RIM, LANES), vmem(2, 2, 2 * RIM, LANES),
            vmem(512, LANES), vmem(3, 128, LANES), vmem(15, 8, LANES),
            dma((4,)), dma((8,)), dma((8,)), dma, dma, dma((3,)), dma((3,)), dma((15,)), dma((15,)),
            dma((15,)), dma((15,)), dma((3,)), dma((3,)), dma, dma, dma((4,)), dma((4,)),
        ],
        compiler_params=pltpu.CompilerParams(collective_id=1, has_side_effects=True, vmem_limit_bytes=16 * 2**20),
        name="collect",
    )(acc, term.reshape(1024, LANES))


def on_device(object_field, probe_field, measured, offsets):
    fixed = [pltpu.with_memory_space_constraint(a, pltpu.HBM) for a in (object_field, measured, probe_field)]
    ext, ordered, probe = exchange(*fixed)
    acc, term = compute(offsets.T, ext, probe, ordered, jnp.asarray(dft_tables(256)))
    return collect(acc, term)


def solution(mesh):
    placed = (P(None, "tile", "pos"), P(), P(("pos", "tile"), None, None), P(("pos", "tile"), None))
    return jax.shard_map(
        on_device,
        mesh=mesh,
        in_specs=placed,
        out_specs=(P(None, "tile", "pos"), P()),
        check_vma=False,
    )
```

```python
import functools
import math

import jax
import jax.numpy as jnp
import numpy as np
from jax import lax
from jax.experimental import pallas as pl
from jax.experimental.pallas import tpu as pltpu
from jax.sharding import PartitionSpec as P

LANES = 128
RIM = 128
F32 = jnp.float32
BF16 = jnp.bfloat16
MESH = pl.DeviceIdType.MESH


def dft_tables(size):
    half = size // 2
    n = np.arange(half)[:, None]
    k = np.arange(half)[None, :]
    out = []
    for parity in range(2):
        phase = (n * (2 * k + parity)) % size
        table = np.exp(-2j * np.pi * phase / size) / math.sqrt(size)
        real = np.block([[table.real, table.imag], [-table.imag, table.real]])
        out += [real, real.T]
    stack = np.stack(out)
    high = stack.astype(np.float32).astype(BF16)
    low = (stack - high.astype(np.float64)).astype(np.float32).astype(BF16)
    return np.stack([high, low], axis=1)


def split(value):
    high = value.astype(BF16)
    return high, (value - high.astype(F32)).astype(BF16)


def dot(a, b):
    return jnp.dot(a, b, preferred_element_type=F32)


def cat(parts, axis):
    return tuple(jnp.concatenate(p, axis=axis) for p in zip(*parts))


def one_position(chunk, row, col, meas, ext_ref, probe_ref, tab_ref, acc_ref, term_ref, rolled):
    size, half = 256, 128
    lane = lax.broadcasted_iota(jnp.int32, (chunk, LANES), 1)
    block = col // LANES
    shift = lax.rem(col, LANES)
    mask = lane >= shift

    def patch(start):
        rows = pl.ds(row + start, chunk)
        out = []
        for plane in range(2):
            b0 = ext_ref[plane, block, rows, :]
            b1 = ext_ref[plane, block + 1, rows, :]
            b2 = ext_ref[plane, block + 2, rows, :]
            out.append((jnp.where(mask, b0, b2), b1))
        return out

    sums, diffs = [], []
    for start in range(0, size, chunk):
        rows = pl.ds(start, chunk)
        (x0r, x1r), (x0i, x1i) = patch(start)
        pr = []
        for plane in range(2):
            r0 = pltpu.roll(probe_ref[plane, 0, rows, :], shift, 1)
            r1 = pltpu.roll(probe_ref[plane, 1, rows, :], shift, 1)
            p0 = jnp.where(mask, r0, r1)
            p1 = jnp.where(mask, r1, r0)
            rolled[plane, 0, rows, :] = p0
            rolled[plane, 1, rows, :] = p1
            pr.append((p0, p1))
        (p0r, p1r), (p0i, p1i) = pr
        e0r = p0r * x0r - p0i * x0i
        e0i = p0r * x0i + p0i * x0r
        e1r = p1r * x1r - p1i * x1i
        e1i = p1r * x1i + p1i * x1r
        sums.append(cat([split(e0r + e1r), split(e0i + e1i)], 1))
        diffs.append(cat([split(e0r - e1r), split(e0i - e1i)], 1))
    a, b = cat(sums, 0), cat(diffs, 0)

    def right(data, index):
        t = tab_ref[index, 0]
        return dot(data[0], t) + dot(data[1], t) + dot(data[0], tab_ref[index, 1])

    def left(index, data):
        t = tab_ref[index, 0]
        return dot(t, data[0]) + dot(t, data[1]) + dot(tab_ref[index, 1], data[0])

    yield
    ye = right(a, 0)
    yo = right(b, 2)
    yield
    s = [y[:half] + y[half:] for y in (ye, yo)]
    d = [y[:half] - y[half:] for y in (ye, yo)]
    a, b = [cat([cat([split(v[:, :LANES]) for v in w], 1), cat([split(v[:, LANES:]) for v in w], 1)], 0)
            for w in (s, d)]
    yield
    ze = left(1, a)
    zo = left(3, b)
    yield
    outs = []
    for z, first in ((ze, 0), (zo, half)):
        zr, zi = z[:half], z[half:]
        power = zr * zr + zi * zi
        factor = 1.0 - meas[pl.ds(first, half), :] * lax.rsqrt(jnp.maximum(power, 1.0))
        outs.append(cat([split(zr * factor), split(zi * factor)], 0))
    a, b = outs
    yield
    e = left(0, a)
    o = left(2, b)
    yield
    s, d = e + o, e - o
    a, b = [cat([cat([split(v[:half, cols]), split(v[half:, cols])], 1) for v in (s, d)], 0)
            for cols in (slice(0, LANES), slice(LANES, 2 * LANES))]
    yield
    e = right(a, 1)
    o = right(b, 3)
    yield
    back_shift = lax.rem(LANES - shift, LANES)
    keep = lane < LANES - shift
    for start in range(0, size, chunk):
        rows = pl.ds(start, chunk)
        ee, oo = e[start:start + chunk], o[start:start + chunk]
        b0, b1 = ee + oo, ee - oo
        b0r, b0i = b0[:, :LANES], b0[:, LANES:]
        b1r, b1i = b1[:, :LANES], b1[:, LANES:]
        p0r, p1r = rolled[0, 0, rows, :], rolled[0, 1, rows, :]
        p0i, p1i = rolled[1, 0, rows, :], rolled[1, 1, rows, :]
        grads = ((p0r * b0r + p0i * b0i, p1r * b1r + p1i * b1i),
                 (p0r * b0i - p0i * b0r, p1r * b1i - p1i * b1r))
        (x0r, x1r), (x0i, x1i) = patch(start)
        dst = pl.ds(row + start, chunk)
        for plane, (g0, g1) in enumerate(grads):
            acc_ref[plane, block, dst, :] += jnp.where(mask, g0, 0.0)
            acc_ref[plane, block + 1, dst, :] += g1
            acc_ref[plane, block + 2, dst, :] += jnp.where(mask, 0.0, g0)
        terms = ((x0r * b0r + x0i * b0i, x1r * b1r + x1i * b1i),
                 (x0r * b0i - x0i * b0r, x1r * b1i - x1i * b1r))
        for plane, (t0, t1) in enumerate(terms):
            r0 = pltpu.roll(t0, back_shift, 1)
            r1 = pltpu.roll(t1, back_shift, 1)
            term_ref[plane, 0, rows, :] += jnp.where(keep, r0, r1)
            term_ref[plane, 1, rows, :] += jnp.where(keep, r1, r0)


def compute_kernel(per_step, chunk, off_ref, ext_ref, probe_ref, meas_ref, tab_ref, acc_ref, term_ref, rolled):
    acc_ref[...] = jnp.zeros_like(acc_ref)
    term_ref[...] = jnp.zeros_like(term_ref)
    stages = 9

    def step(index, carry):
        live = []
        for slot in range(per_step):
            pos = index * per_step + slot
            row = lax.rem(off_ref[0, pos] + 128, 256)
            col = lax.rem(off_ref[1, pos] + 128, 512)
            live.append(one_position(chunk, row, col, meas_ref.at[pos], ext_ref, probe_ref, tab_ref,
                                     acc_ref, term_ref, rolled.at[slot]))
        for tick in range(stages + per_step - 1):
            for slot, gen in enumerate(live):
                if 0 <= tick - slot < stages:
                    next(gen, None)
        return carry

    lax.fori_loop(0, meas_ref.shape[0] // per_step, step, 0)


def compute(offsets, ext, probe, meas, tables, per_step=4, chunk=32):
    vmem = pl.BlockSpec(memory_space=pltpu.VMEM)
    return pl.pallas_call(
        functools.partial(compute_kernel, per_step, chunk),
        in_specs=[pl.BlockSpec(memory_space=pltpu.SMEM)] + [vmem] * 4,
        out_specs=[vmem] * 2,
        out_shape=[jax.ShapeDtypeStruct(ext.shape, F32), jax.ShapeDtypeStruct(probe.shape, F32)],
        scratch_shapes=[pltpu.VMEM((per_step, 2, 2, 256, 128), F32)],
        compiler_params=pltpu.CompilerParams(vmem_limit_bytes=32 * 2**20),
        name="updates",
    )(offsets, ext, probe, meas, tables)


POS, TILE = "pos", "tile"


def neighbour(dy, dx):
    p, t = lax.axis_index(POS), lax.axis_index(TILE)
    tp, tt = p + dx, t + dy
    inside = (tp >= 0) & (tp < lax.axis_size(POS)) & (tt >= 0) & (tt < lax.axis_size(TILE))
    return (tp, tt), inside


def greet(peers):
    barrier = pltpu.get_barrier_semaphore()
    for device, inside in peers:
        @pl.when(inside)
        def _():
            pl.semaphore_signal(barrier, inc=1, device_id=device, device_id_type=MESH)
    pl.semaphore_wait(barrier, sum(inside.astype(jnp.int32) for _, inside in peers))


def chip_side():
    core = lax.rem(lax.axis_index(TILE), 2)
    inner = 1 - 2 * core
    return core, inner, (lax.axis_index(POS), lax.axis_index(TILE) + inner)


def remote(src, dst, send, recv, device):
    return pltpu.make_async_remote_copy(src_ref=src, dst_ref=dst, send_sem=send, recv_sem=recv,
                                        device_id=device, device_id_type=MESH)


def when_each(condition, *calls):
    @pl.when(condition)
    def _():
        for call in calls:
            call()


def order_table(rows_first, size):
    out = lax.broadcasted_iota(jnp.int32, (size, size), 0 if rows_first else 1)
    src = lax.broadcasted_iota(jnp.int32, (size, size), 1 if rows_first else 0)
    half = size // 2
    wanted = jnp.where(out < half, 2 * out, 2 * out - size + 1)
    return jnp.where(src == wanted, 1.0, 0.0).astype(BF16)


def halo_kernel(obj_ref, meas_ref, prb_ref, ext_ref, out_ref, probe_ref, zeros, loaded, ordered, send_sem, recv_sem,
                fill_sem, own_sem, in_sem, out_sem, relay_send, relay_recv, probe_sem):
    group = loaded.shape[0] // in_sem.shape[0]
    size = loaded.shape[1]
    core, inner, partner = chip_side()
    p, t = lax.axis_index(POS), lax.axis_index(TILE)
    loads = [pltpu.make_async_copy(meas_ref.at[pl.ds(g * group, group)], loaded.at[pl.ds(g * group, group)], in_sem.at[g])
             for g in range(in_sem.shape[0])]
    locals_ = [pltpu.make_async_copy(obj_ref.at[:, :, pl.ds(b * LANES, LANES)], ext_ref.at[:, b + 1, pl.ds(RIM, 2 * RIM), :],
                                     own_sem.at[b]) for b in range(4)]
    locals_ += [pltpu.make_async_copy(prb_ref.at[:, :, pl.ds(b * LANES, LANES)], probe_ref.at[:, b], probe_sem.at[b])
                for b in range(2)]
    sides = [neighbour(0, -1), neighbour(0, 1)]
    outer, outer_in = neighbour(-inner, 0)
    corners = [neighbour(-inner, -1), neighbour(-inner, 1)]
    for load in loads:
        load.start()
    greet(sides + corners + [(outer, outer_in), (partner, p >= 0)])
    inner_row = pl.multiple_of((1 - core) * RIM, RIM)
    outer_row = pl.multiple_of(core * RIM, RIM)
    inner_halo = pl.multiple_of((1 - core) * 3 * RIM, RIM)
    outer_halo = pl.multiple_of(core * 3 * RIM, RIM)
    pairs = []

    def add(src_row, count, block, dst_block, dst_row, device, there, source_there, fill_row):
        index = len(pairs)
        copy = remote(obj_ref.at[:, pl.ds(src_row, count), pl.ds(block * LANES, LANES)],
                      ext_ref.at[:, dst_block, pl.ds(dst_row, count), :], send_sem.at[index], recv_sem.at[index], device)
        fill = pltpu.make_async_copy(zeros.at[:, pl.ds(0, count), :], ext_ref.at[:, dst_block, pl.ds(fill_row, count), :],
                                     fill_sem.at[index])
        pairs.append((copy, there, source_there, fill))
        when_each(there, copy.start)

    add(0, 2 * RIM, 0, 5, RIM, sides[0][0], sides[0][1], sides[1][1], RIM)
    add(0, 2 * RIM, 3, 0, RIM, sides[1][0], sides[1][1], sides[0][1], RIM)
    there_row = pl.multiple_of((1 - core) * 3 * RIM, RIM)
    for b in range(4):
        add(outer_row, RIM, b, b + 1, there_row, outer, outer_in, outer_in, outer_halo)
    add(outer_row, RIM, 0, 5, there_row, corners[0][0], corners[0][1], corners[1][1], outer_halo)
    add(outer_row, RIM, 3, 0, there_row, corners[1][0], corners[1][1], corners[0][1], outer_halo)
    partner_halo = pl.multiple_of(core * 3 * RIM, RIM)
    inside = [remote(obj_ref.at[:, pl.ds(inner_row, RIM), pl.ds(b * LANES, LANES)],
                     ext_ref.at[:, b + 1, pl.ds(partner_halo, RIM), :], relay_send.at[b], relay_recv.at[b], partner)
              for b in range(4)]
    for copy in inside:
        copy.start()
    for copy in locals_:
        copy.start()
    zeros[...] = jnp.zeros_like(zeros)
    for copy, there, source_there, fill in pairs:
        when_each(jnp.logical_not(source_there), fill.start)
    perm_rows, perm_cols = order_table(True, size), order_table(False, size)
    stores = []

    def relay():
        made = []
        inner_own = pl.multiple_of((2 - core) * RIM, RIM)
        for k, block in enumerate((5, 0)):
            copy, there, source_there, fill = pairs[k]
            when_each(source_there, copy.wait_recv)
            when_each(jnp.logical_not(source_there), fill.wait)
            here = ext_ref.at[:, block, pl.ds(inner_own, RIM), :]
            there_ref = ext_ref.at[:, block, pl.ds(partner_halo, RIM), :]
            made.append(remote(here, there_ref, relay_send.at[4 + k], relay_recv.at[4 + k], partner))
            made[-1].start()
        return made

    for g in range(in_sem.shape[0]):
        loads[g].wait()

        def order(i, carry):
            at = g * group + 2 * i
            parts = [split(loaded[at + j]) for j in range(2)]
            done = None
            for k in range(2):
                rows = jnp.concatenate([parts[0][k], parts[1][k]], axis=0)
                moved = dot(rows, perm_cols).astype(BF16)
                moved = jnp.concatenate([moved[:size], moved[size:]], axis=1)
                moved = dot(perm_rows, moved)
                done = moved if done is None else done + moved
            ordered[at] = done[:, :size]
            ordered[at + 1] = done[:, size:]
            return carry

        lax.fori_loop(0, group // 2, order, 0)
        store = pltpu.make_async_copy(ordered.at[pl.ds(g * group, group)], out_ref.at[pl.ds(g * group, group)], out_sem.at[g])
        store.start()
        stores.append(store)
    inside += relay()
    for copy in stores + locals_:
        copy.wait()
    for index, (copy, there, source_there, fill) in enumerate(pairs):
        when_each(there, copy.wait_send)
        if index >= 2:
            when_each(source_there, copy.wait_recv)
            when_each(jnp.logical_not(source_there), fill.wait)
    for copy in inside:
        copy.wait()


def exchange(object_field, measured, probe_field):
    groups = 4
    dma = pltpu.SemaphoreType.DMA
    anywhere = pl.BlockSpec(memory_space=pl.ANY)
    return pl.pallas_call(
        halo_kernel,
        in_specs=[pl.BlockSpec(memory_space=pltpu.HBM)] * 3,
        out_specs=[anywhere] * 3,
        out_shape=[jax.ShapeDtypeStruct((2, 6, 4 * RIM, LANES), F32), jax.ShapeDtypeStruct(measured.shape, F32),
                   jax.ShapeDtypeStruct((2, 2, 2 * RIM, LANES), F32)],
        scratch_shapes=[
            pltpu.VMEM((2, 2 * RIM, LANES), F32),
            pltpu.VMEM(measured.shape, F32),
            pltpu.VMEM(measured.shape, F32),
            dma((8,)), dma((8,)), dma((8,)),
            dma((4,)), dma((groups,)), dma((groups,)), dma((6,)), dma((6,)), dma((2,)),
        ],
        compiler_params=pltpu.CompilerParams(collective_id=0, has_side_effects=True, vmem_limit_bytes=16 * 2**20),
        name="halo",
    )(object_field, measured, probe_field)


def gather_kernel(acc_ref, term_ref, obj_ref, probe_ref, own, total, result, *rest):
    (recv_v, recv_in, recv_c, recv_h, recv_d, side, part1, part2, part3,
     load_sem, send_sem, recv_sem, s1, r1, s2, r2, s3, r3, s4, r4, s5, r5, s6, r6, out_sem, pout_sem) = rest
    p, t = lax.axis_index(POS), lax.axis_index(TILE)
    x, z = p // 4, lax.rem(p, 4)
    y = t // 2
    core, inner, partner = chip_side()
    yz = y * 4 + z
    yes = p >= 0
    x_peers = [(lax.rem(x + k, 4) * 4 + z, t) for k in range(1, 4)]
    x_ids = [lax.rem(x + k, 4) for k in range(1, 4)]
    yz_ids = [lax.rem(yz + k, 16) for k in range(1, 16)]
    yz_peers = [(x * 4 + lax.rem(i, 4), (i // 4) * 2 + core) for i in yz_ids]
    sides = [neighbour(0, -1), neighbour(0, 1)]
    outer, outer_in = neighbour(-inner, 0)
    corners = [neighbour(-inner, -1), neighbour(-inner, 1)]

    load_total = pltpu.make_async_copy(term_ref, total, load_sem.at[0])
    load_own = pltpu.make_async_copy(acc_ref.at[:, pl.ds(1, 4), pl.ds(RIM, 2 * RIM), :], own, load_sem.at[1])
    load_sides = [pltpu.make_async_copy(acc_ref.at[:, b, pl.ds(RIM, 2 * RIM), :], side.at[k], load_sem.at[2 + k])
                  for k, b in enumerate((0, 5))]
    load_total.start()
    for load in load_sides:
        load.start()
    load_own.start()
    greet([(partner, yes), (outer, outer_in)] + sides + corners + [(d, yes) for d in x_peers] + [(d, yes) for d in yz_peers])
    load_total.wait()
    half = 512
    mine = pl.multiple_of(core * half, half)
    other = pl.multiple_of((1 - core) * half, half)
    quarter = half // 4
    order = x_ids + [x]
    firsts = [remote(total.at[pl.ds(pl.multiple_of(other + i * quarter, quarter), quarter)], part1.at[k], s1.at[k], r1.at[k], partner)
              for k, i in enumerate(order)]
    for c in firsts:
        c.start()
    inner_halo = pl.multiple_of((1 - core) * 3 * RIM, RIM)
    outer_halo = pl.multiple_of(core * 3 * RIM, RIM)
    count = 0

    def link(src, dst, device):
        nonlocal count
        copy = remote(src, dst, send_sem.at[count], recv_sem.at[count], device)
        count += 1
        return copy

    inner_corners = [link(acc_ref.at[:, b, pl.ds(inner_halo, RIM), :], recv_c.at[k], partner) for k, b in enumerate((0, 5))]
    for copy in inner_corners:
        copy.start()
    inner_main = link(acc_ref.at[:, pl.ds(1, 4), pl.ds(inner_halo, RIM), :], recv_in, partner)
    outer_main = link(acc_ref.at[:, pl.ds(1, 4), pl.ds(outer_halo, RIM), :], recv_v, outer)
    diagonal = [link(acc_ref.at[:, b, pl.ds(outer_halo, RIM), :], recv_d.at[k], corners[k][0]) for k, b in enumerate((0, 5))]
    across = [link(side.at[k], recv_h.at[k], sides[k][0]) for k in range(2)]
    when_each(outer_in, outer_main.start)
    seconds = []
    for k, i in enumerate(order):
        firsts[k].wait_recv()
        rows = pl.ds(pl.multiple_of(mine + i * quarter, quarter), quarter)
        total[rows] = total[rows] + part1[k]
        if k < 3:
            seconds.append(remote(total.at[rows], part2.at[k], s2.at[k], r2.at[k], x_peers[k]))
            seconds[k].start()
    inner_main.start()
    near = pl.multiple_of((1 - core) * RIM, RIM)
    for k in range(2):
        inner_corners[k].wait()
        load_sides[k].wait()
        side[k, :, pl.ds(near, RIM), :] = side[k, :, pl.ds(near, RIM), :] + recv_c[k]
        when_each(sides[k][1], across[k].start)
    at2 = pl.multiple_of(mine + x * quarter, quarter)
    for c in seconds:
        c.wait_recv()
    total[pl.ds(at2, quarter)] = total[pl.ds(at2, quarter)] + part2[0] + part2[1] + part2[2]
    piece = quarter // 16
    thirds = [remote(total.at[pl.ds(pl.multiple_of(at2 + i * piece, piece), piece)], part3.at[k], s3.at[k], r3.at[k], d)
              for k, (i, d) in enumerate(zip(yz_ids, yz_peers))]
    for c in thirds:
        c.start()
    load_own.wait()
    far = pl.multiple_of(core * RIM, RIM)
    inner_main.wait()

    def add_rows(src, at):
        def body(i, carry):
            plane, b = i // 4, lax.rem(i, 4)
            own[plane, b, pl.ds(at, RIM), :] = own[plane, b, pl.ds(at, RIM), :] + src[plane, b]
            return carry
        lax.fori_loop(0, 8, body, 0)

    add_rows(recv_in, near)
    for c in thirds:
        c.wait_recv()
    at3 = pl.multiple_of(at2 + yz * piece, piece)
    value = total[pl.ds(at3, piece)]
    for k in range(15):
        value = value + part3[k]
    result[pl.ds(at3, piece)] = value * (1.0 / math.sqrt(2048))
    here = result.at[pl.ds(at3, piece)]
    fourths = [remote(here, here, s4.at[k], r4.at[k], d) for k, d in enumerate(yz_peers)]
    for c in fourths:
        c.start()

    @pl.when(outer_in)
    def _():
        outer_main.wait()
        add_rows(recv_v, far)

    outs = [pltpu.make_async_copy(own.at[:, b], obj_ref.at[:, :, pl.ds(b * LANES, LANES)], out_sem.at[b]) for b in range(4)]
    for b in (1, 2):
        outs[b].start()
    for c in fourths:
        c.wait_recv()
    here2 = result.at[pl.ds(at2, quarter)]
    fifths = [remote(here2, here2, s5.at[k], r5.at[k], d) for k, d in enumerate(x_peers)]
    for c in fifths:
        c.start()
    lasts = [remote(here2, here2, s6.at[3], r6.at[3], partner)]
    lasts[0].start()
    for k in range(2):
        when_each(corners[k][1], diagonal[k].start)
    for k in range(2):
        block = 3 - 3 * k
        source, diagonal_source = sides[1 - k][1], corners[1 - k][1]

        @pl.when(source)
        def _():
            across[k].wait_recv()
            own[:, block] = own[:, block] + recv_h[k]

        @pl.when(diagonal_source)
        def _():
            diagonal[k].wait_recv()
            own[:, block, pl.ds(far, RIM), :] = own[:, block, pl.ds(far, RIM), :] + recv_d[k]

        outs[block].start()
    for k, c in enumerate(fifths):
        c.wait_recv()
        from_x = lax.rem(x + 3 - k, 4)
        here1 = result.at[pl.ds(pl.multiple_of(mine + from_x * quarter, quarter), quarter)]
        lasts.append(remote(here1, here1, s6.at[k], r6.at[k], partner))
        lasts[-1].start()
    for plane, ready in ((core, ()), (1 - core, lasts)):
        for c in ready:
            c.wait_recv()
        for b in range(2):
            rows = pl.ds(pl.multiple_of(plane * half + b * (half // 2), half // 2), half // 2)
            out = pltpu.make_async_copy(result.at[rows], probe_ref.at[plane, :, pl.ds(b * LANES, LANES)], pout_sem.at[len(outs) - 4])
            out.start()
            outs.append(out)
    for c in firsts + seconds + thirds + fourths + fifths + lasts:
        c.wait_send()
    for k in range(2):
        when_each(sides[k][1], across[k].wait_send)
        when_each(corners[k][1], diagonal[k].wait_send)
    for out in outs:
        out.wait()


def collect(acc, term):
    dma = pltpu.SemaphoreType.DMA
    vmem = lambda *shape: pltpu.VMEM(shape, F32)
    return pl.pallas_call(
        gather_kernel,
        in_specs=[pl.BlockSpec(memory_space=pl.ANY)] * 2,
        out_specs=[pl.BlockSpec(memory_space=pl.ANY)] * 2,
        out_shape=[jax.ShapeDtypeStruct((2, 256, 512), F32), jax.ShapeDtypeStruct((2, 256, 256), F32)],
        scratch_shapes=[
            vmem(2, 4, 2 * RIM, LANES), vmem(1024, LANES), vmem(1024, LANES),
            vmem(2, 4, RIM, LANES), vmem(2, 4, RIM, LANES), vmem(2, 2, RIM, LANES), vmem(2, 2, 2 * RIM, LANES),
            vmem(2, 2, RIM, LANES), vmem(2, 2, 2 * RIM, LANES),
            vmem(4, 128, LANES), vmem(3, 128, LANES), vmem(15, 8, LANES),
            dma((4,)), dma((8,)), dma((8,)), dma((4,)), dma((4,)), dma((3,)), dma((3,)), dma((15,)), dma((15,)),
            dma((15,)), dma((15,)), dma((3,)), dma((3,)), dma((4,)), dma((4,)), dma((4,)), dma((4,)),
        ],
        compiler_params=pltpu.CompilerParams(collective_id=1, has_side_effects=True, vmem_limit_bytes=16 * 2**20),
        name="collect",
    )(acc, term.reshape(1024, LANES))


def on_device(object_field, probe_field, measured, offsets):
    fixed = [pltpu.with_memory_space_constraint(a, pltpu.HBM) for a in (object_field, measured, probe_field)]
    ext, ordered, probe = exchange(*fixed)
    acc, term = compute(offsets.T, ext, probe, ordered, jnp.asarray(dft_tables(256)))
    return collect(acc, term)


def solution(mesh):
    placed = (P(None, "tile", "pos"), P(), P(("pos", "tile"), None, None), P(("pos", "tile"), None))
    return jax.shard_map(
        on_device,
        mesh=mesh,
        in_specs=placed,
        out_specs=(P(None, "tile", "pos"), P()),
        check_vma=False,
    )
```

```python
import functools
import math

import jax
import jax.numpy as jnp
import numpy as np
from jax import lax
from jax.experimental import pallas as pl
from jax.experimental.pallas import tpu as pltpu
from jax.sharding import PartitionSpec as P

LANES = 128
RIM = 128
F32 = jnp.float32
BF16 = jnp.bfloat16
MESH = pl.DeviceIdType.MESH


def dft_tables(size):
    half = size // 2
    n = np.arange(half)[:, None]
    k = np.arange(half)[None, :]
    out = []
    for parity in range(2):
        phase = (n * (2 * k + parity)) % size
        table = np.exp(-2j * np.pi * phase / size) / math.sqrt(size)
        real = np.block([[table.real, table.imag], [-table.imag, table.real]])
        out += [real, real.T]
    stack = np.stack(out)
    high = stack.astype(np.float32).astype(BF16)
    low = (stack - high.astype(np.float64)).astype(np.float32).astype(BF16)
    return np.stack([high, low], axis=1)


def row_tables(size):
    quarter = size // 4
    n = np.arange(quarter)[:, None]
    k = np.arange(quarter)[None, :]
    out = []
    for residue in range(4):
        phase = (n * (4 * k + residue)) % size
        table = np.exp(-2j * np.pi * phase / size) / math.sqrt(size)
        real = np.block([[table.real, table.imag], [-table.imag, table.real]])
        out.append([real.T, real])
    stack = np.array(out).transpose(1, 0, 2, 3)
    high = stack.astype(np.float32).astype(BF16)
    low = (stack - high.astype(np.float64)).astype(np.float32).astype(BF16)
    both = np.concatenate([high, high], axis=-1)
    return np.concatenate([both, np.concatenate([low, np.zeros_like(low)], axis=-1)], axis=2)


def split(value):
    high = value.astype(BF16)
    return high, (value - high.astype(F32)).astype(BF16)


def dot(a, b):
    return jnp.dot(a, b, preferred_element_type=F32)


def cat(parts, axis):
    return tuple(jnp.concatenate(p, axis=axis) for p in zip(*parts))


def one_position(chunk, row, col, meas, ext_ref, probe_ref, tab_ref, rtab_ref, acc_ref, term_ref, rolled):
    size, half = 256, 128
    lane = lax.broadcasted_iota(jnp.int32, (chunk, LANES), 1)
    block = col // LANES
    shift = lax.rem(col, LANES)
    mask = lane >= shift

    def patch(start):
        rows = pl.ds(row + start, chunk)
        out = []
        for plane in range(2):
            b0 = ext_ref[plane, block, rows, :]
            b1 = ext_ref[plane, block + 1, rows, :]
            b2 = ext_ref[plane, block + 2, rows, :]
            out.append((jnp.where(mask, b0, b2), b1))
        return out

    sums, diffs = [], []
    for start in range(0, size, chunk):
        rows = pl.ds(start, chunk)
        (x0r, x1r), (x0i, x1i) = patch(start)
        pr = []
        for plane in range(2):
            r0 = pltpu.roll(probe_ref[plane, 0, rows, :], shift, 1)
            r1 = pltpu.roll(probe_ref[plane, 1, rows, :], shift, 1)
            p0 = jnp.where(mask, r0, r1)
            p1 = jnp.where(mask, r1, r0)
            rolled[plane, 0, rows, :] = p0
            rolled[plane, 1, rows, :] = p1
            pr.append((p0, p1))
        (p0r, p1r), (p0i, p1i) = pr
        e0r = p0r * x0r - p0i * x0i
        e0i = p0r * x0i + p0i * x0r
        e1r = p1r * x1r - p1i * x1i
        e1i = p1r * x1i + p1i * x1r
        sums.append(cat([split(e0r + e1r), split(e0i + e1i)], 1))
        diffs.append(cat([split(e0r - e1r), split(e0i - e1i)], 1))
    a, b = cat(sums, 0), cat(diffs, 0)

    def right(data, index):
        t = tab_ref[index, 0]
        return dot(data[0], t) + dot(data[1], t) + dot(data[0], tab_ref[index, 1])

    def left(inverse, residue, stacked):
        product = dot(rtab_ref[inverse, residue], stacked)
        return product[:size // 2] + product[size // 2:]

    def stack(real, imag):
        (rh, rl), (ih, il) = split(real), split(imag)
        return jnp.concatenate([rh, ih, rl, il], axis=0)

    yield
    ye = right(a, 0)
    yo = right(b, 2)
    yield
    quarter = size // 4

    def both(part, m):
        rows = slice(m * quarter, (m + 1) * quarter)
        cols = slice(part * LANES, (part + 1) * LANES)
        return jnp.concatenate([ye[rows, cols], yo[rows, cols]], axis=1)

    re, im = [[both(part, m) for m in range(4)] for part in range(2)]
    t0, t1, t2, t3 = [(re[0] + re[2], im[0] + im[2]), (re[0] - re[2], im[0] - im[2]),
                      (re[1] + re[3], im[1] + im[3]), (re[1] - re[3], im[1] - im[3])]
    inputs = [stack(t0[0] + t2[0], t0[1] + t2[1]), stack(t1[0] + t3[1], t1[1] - t3[0]),
              stack(t0[0] - t2[0], t0[1] - t2[1]), stack(t1[0] - t3[1], t1[1] + t3[0])]
    yield
    waves = [left(0, q, inputs[q]) for q in range(4)]
    yield
    inputs = []
    for q, z in enumerate(waves):
        zr, zi = z[:quarter], z[quarter:]
        power = zr * zr + zi * zi
        factor = 1.0 - meas[pl.ds(q * quarter, quarter), :] * lax.rsqrt(jnp.maximum(power, 1.0))
        inputs.append(stack(zr * factor, zi * factor))
    yield
    v = [left(1, q, inputs[q]) for q in range(4)]
    v = [(w[:quarter], w[quarter:]) for w in v]
    yield
    (s0r, s1r, s2r, s3r), (s0i, s1i, s2i, s3i) = [
        (v[0][c] + v[2][c], v[0][c] - v[2][c], v[1][c] + v[3][c], v[1][c] - v[3][c]) for c in range(2)]
    outs = [(s0r + s2r, s0i + s2i), (s1r - s3i, s1i + s3r), (s0r - s2r, s0i - s2i), (s1r + s3i, s1i - s3r)]
    a, b = [cat([cat([split(xr[:, cols]), split(xi[:, cols])], 1) for xr, xi in outs], 0)
            for cols in (slice(0, LANES), slice(LANES, 2 * LANES))]
    yield
    e = right(a, 1)
    o = right(b, 3)
    yield
    back_shift = lax.rem(LANES - shift, LANES)
    keep = lane < LANES - shift
    for start in range(0, size, chunk):
        rows = pl.ds(start, chunk)
        ee, oo = e[start:start + chunk], o[start:start + chunk]
        b0, b1 = ee + oo, ee - oo
        b0r, b0i = b0[:, :LANES], b0[:, LANES:]
        b1r, b1i = b1[:, :LANES], b1[:, LANES:]
        p0r, p1r = rolled[0, 0, rows, :], rolled[0, 1, rows, :]
        p0i, p1i = rolled[1, 0, rows, :], rolled[1, 1, rows, :]
        grads = ((p0r * b0r + p0i * b0i, p1r * b1r + p1i * b1i),
                 (p0r * b0i - p0i * b0r, p1r * b1i - p1i * b1r))
        (x0r, x1r), (x0i, x1i) = patch(start)
        dst = pl.ds(row + start, chunk)
        for plane, (g0, g1) in enumerate(grads):
            acc_ref[plane, block, dst, :] += jnp.where(mask, g0, 0.0)
            acc_ref[plane, block + 1, dst, :] += g1
            acc_ref[plane, block + 2, dst, :] += jnp.where(mask, 0.0, g0)
        terms = ((x0r * b0r + x0i * b0i, x1r * b1r + x1i * b1i),
                 (x0r * b0i - x0i * b0r, x1r * b1i - x1i * b1r))
        for plane, (t0, t1) in enumerate(terms):
            r0 = pltpu.roll(t0, back_shift, 1)
            r1 = pltpu.roll(t1, back_shift, 1)
            term_ref[plane, 0, rows, :] += jnp.where(keep, r0, r1)
            term_ref[plane, 1, rows, :] += jnp.where(keep, r1, r0)


def compute_kernel(per_step, chunk, off_ref, ext_ref, probe_ref, meas_ref, tab_ref, rtab_ref, acc_ref, term_ref, rolled):
    acc_ref[...] = jnp.zeros_like(acc_ref)
    term_ref[...] = jnp.zeros_like(term_ref)
    stages = 9

    def step(index, carry):
        live = []
        for slot in range(per_step):
            pos = index * per_step + slot
            row = lax.rem(off_ref[0, pos] + 128, 256)
            col = lax.rem(off_ref[1, pos] + 128, 512)
            live.append(one_position(chunk, row, col, meas_ref.at[pos], ext_ref, probe_ref, tab_ref, rtab_ref,
                                     acc_ref, term_ref, rolled.at[slot]))
        for tick in range(stages + per_step - 1):
            for slot, gen in enumerate(live):
                if 0 <= tick - slot < stages:
                    next(gen, None)
        return carry

    lax.fori_loop(0, meas_ref.shape[0] // per_step, step, 0)


def compute(offsets, ext, probe, meas, tables, rows, per_step=4, chunk=32):
    vmem = pl.BlockSpec(memory_space=pltpu.VMEM)
    return pl.pallas_call(
        functools.partial(compute_kernel, per_step, chunk),
        in_specs=[pl.BlockSpec(memory_space=pltpu.SMEM)] + [vmem] * 5,
        out_specs=[vmem] * 2,
        out_shape=[jax.ShapeDtypeStruct(ext.shape, F32), jax.ShapeDtypeStruct(probe.shape, F32)],
        scratch_shapes=[pltpu.VMEM((per_step, 2, 2, 256, 128), F32)],
        compiler_params=pltpu.CompilerParams(vmem_limit_bytes=32 * 2**20),
        name="updates",
    )(offsets, ext, probe, meas, tables, rows)


POS, TILE = "pos", "tile"


def neighbour(dy, dx):
    p, t = lax.axis_index(POS), lax.axis_index(TILE)
    tp, tt = p + dx, t + dy
    inside = (tp >= 0) & (tp < lax.axis_size(POS)) & (tt >= 0) & (tt < lax.axis_size(TILE))
    return (tp, tt), inside


def greet(peers):
    barrier = pltpu.get_barrier_semaphore()
    for device, inside in peers:
        @pl.when(inside)
        def _():
            pl.semaphore_signal(barrier, inc=1, device_id=device, device_id_type=MESH)
    pl.semaphore_wait(barrier, sum(inside.astype(jnp.int32) for _, inside in peers))


def chip_side():
    core = lax.rem(lax.axis_index(TILE), 2)
    inner = 1 - 2 * core
    return core, inner, (lax.axis_index(POS), lax.axis_index(TILE) + inner)


def remote(src, dst, send, recv, device):
    return pltpu.make_async_remote_copy(src_ref=src, dst_ref=dst, send_sem=send, recv_sem=recv,
                                        device_id=device, device_id_type=MESH)


def when_each(condition, *calls):
    @pl.when(condition)
    def _():
        for call in calls:
            call()


def order_table(rows_first, size):
    out = lax.broadcasted_iota(jnp.int32, (size, size), 0 if rows_first else 1)
    src = lax.broadcasted_iota(jnp.int32, (size, size), 1 if rows_first else 0)
    radix = 4 if rows_first else 2
    wanted = lax.rem(out, size // radix) * radix + out // (size // radix)
    return jnp.where(src == wanted, 1.0, 0.0).astype(BF16)


def halo_kernel(obj_ref, meas_ref, prb_ref, ext_ref, out_ref, probe_ref, zeros, loaded, ordered, send_sem, recv_sem,
                fill_sem, own_sem, in_sem, out_sem, relay_send, relay_recv, probe_sem):
    group = loaded.shape[0] // in_sem.shape[0]
    size = loaded.shape[1]
    core, inner, partner = chip_side()
    p, t = lax.axis_index(POS), lax.axis_index(TILE)
    loads = [pltpu.make_async_copy(meas_ref.at[pl.ds(g * group, group)], loaded.at[pl.ds(g * group, group)], in_sem.at[g])
             for g in range(in_sem.shape[0])]
    locals_ = [pltpu.make_async_copy(obj_ref.at[:, :, pl.ds(b * LANES, LANES)], ext_ref.at[:, b + 1, pl.ds(RIM, 2 * RIM), :],
                                     own_sem.at[b]) for b in range(4)]
    locals_ += [pltpu.make_async_copy(prb_ref.at[:, :, pl.ds(b * LANES, LANES)], probe_ref.at[:, b], probe_sem.at[b])
                for b in range(2)]
    sides = [neighbour(0, -1), neighbour(0, 1)]
    outer, outer_in = neighbour(-inner, 0)
    corners = [neighbour(-inner, -1), neighbour(-inner, 1)]
    for load in loads:
        load.start()
    greet(sides + corners + [(outer, outer_in), (partner, p >= 0)])
    inner_row = pl.multiple_of((1 - core) * RIM, RIM)
    outer_row = pl.multiple_of(core * RIM, RIM)
    inner_halo = pl.multiple_of((1 - core) * 3 * RIM, RIM)
    outer_halo = pl.multiple_of(core * 3 * RIM, RIM)
    pairs = []

    def add(src_row, count, block, dst_block, dst_row, device, there, source_there, fill_row):
        index = len(pairs)
        copy = remote(obj_ref.at[:, pl.ds(src_row, count), pl.ds(block * LANES, LANES)],
                      ext_ref.at[:, dst_block, pl.ds(dst_row, count), :], send_sem.at[index], recv_sem.at[index], device)
        fill = pltpu.make_async_copy(zeros.at[:, pl.ds(0, count), :], ext_ref.at[:, dst_block, pl.ds(fill_row, count), :],
                                     fill_sem.at[index])
        pairs.append((copy, there, source_there, fill))
        when_each(there, copy.start)

    add(0, 2 * RIM, 0, 5, RIM, sides[0][0], sides[0][1], sides[1][1], RIM)
    add(0, 2 * RIM, 3, 0, RIM, sides[1][0], sides[1][1], sides[0][1], RIM)
    there_row = pl.multiple_of((1 - core) * 3 * RIM, RIM)
    for b in range(4):
        add(outer_row, RIM, b, b + 1, there_row, outer, outer_in, outer_in, outer_halo)
    add(outer_row, RIM, 0, 5, there_row, corners[0][0], corners[0][1], corners[1][1], outer_halo)
    add(outer_row, RIM, 3, 0, there_row, corners[1][0], corners[1][1], corners[0][1], outer_halo)
    partner_halo = pl.multiple_of(core * 3 * RIM, RIM)
    inside = [remote(obj_ref.at[:, pl.ds(inner_row, RIM), pl.ds(b * LANES, LANES)],
                     ext_ref.at[:, b + 1, pl.ds(partner_halo, RIM), :], relay_send.at[b], relay_recv.at[b], partner)
              for b in range(4)]
    for copy in inside:
        copy.start()
    for copy in locals_:
        copy.start()
    zeros[...] = jnp.zeros_like(zeros)
    for copy, there, source_there, fill in pairs:
        when_each(jnp.logical_not(source_there), fill.start)
    perm_rows, perm_cols = order_table(True, size), order_table(False, size)
    stores = []

    def relay():
        made = []
        inner_own = pl.multiple_of((2 - core) * RIM, RIM)
        for k, block in enumerate((5, 0)):
            copy, there, source_there, fill = pairs[k]
            when_each(source_there, copy.wait_recv)
            when_each(jnp.logical_not(source_there), fill.wait)
            here = ext_ref.at[:, block, pl.ds(inner_own, RIM), :]
            there_ref = ext_ref.at[:, block, pl.ds(partner_halo, RIM), :]
            made.append(remote(here, there_ref, relay_send.at[4 + k], relay_recv.at[4 + k], partner))
            made[-1].start()
        return made

    for g in range(in_sem.shape[0]):
        loads[g].wait()

        def order(i, carry):
            at = g * group + 2 * i
            parts = [split(loaded[at + j]) for j in range(2)]
            done = None
            for k in range(2):
                rows = jnp.concatenate([parts[0][k], parts[1][k]], axis=0)
                moved = dot(rows, perm_cols).astype(BF16)
                moved = jnp.concatenate([moved[:size], moved[size:]], axis=1)
                moved = dot(perm_rows, moved)
                done = moved if done is None else done + moved
            ordered[at] = done[:, :size]
            ordered[at + 1] = done[:, size:]
            return carry

        lax.fori_loop(0, group // 2, order, 0)
        store = pltpu.make_async_copy(ordered.at[pl.ds(g * group, group)], out_ref.at[pl.ds(g * group, group)], out_sem.at[g])
        store.start()
        stores.append(store)
    inside += relay()
    for copy in stores + locals_:
        copy.wait()
    for index, (copy, there, source_there, fill) in enumerate(pairs):
        when_each(there, copy.wait_send)
        if index >= 2:
            when_each(source_there, copy.wait_recv)
            when_each(jnp.logical_not(source_there), fill.wait)
    for copy in inside:
        copy.wait()


def exchange(object_field, measured, probe_field):
    groups = 4
    dma = pltpu.SemaphoreType.DMA
    anywhere = pl.BlockSpec(memory_space=pl.ANY)
    return pl.pallas_call(
        halo_kernel,
        in_specs=[pl.BlockSpec(memory_space=pltpu.HBM)] * 3,
        out_specs=[anywhere] * 3,
        out_shape=[jax.ShapeDtypeStruct((2, 6, 4 * RIM, LANES), F32), jax.ShapeDtypeStruct(measured.shape, F32),
                   jax.ShapeDtypeStruct((2, 2, 2 * RIM, LANES), F32)],
        scratch_shapes=[
            pltpu.VMEM((2, 2 * RIM, LANES), F32),
            pltpu.VMEM(measured.shape, F32),
            pltpu.VMEM(measured.shape, F32),
            dma((8,)), dma((8,)), dma((8,)),
            dma((4,)), dma((groups,)), dma((groups,)), dma((6,)), dma((6,)), dma((2,)),
        ],
        compiler_params=pltpu.CompilerParams(collective_id=0, has_side_effects=True, vmem_limit_bytes=16 * 2**20),
        name="halo",
    )(object_field, measured, probe_field)


def gather_kernel(acc_ref, term_ref, own, result, total, *rest):
    (recv_v, recv_in, recv_c, recv_h, recv_d, side, part1, part2, part3,
     load_sem, send_sem, recv_sem, s1, r1, s2, r2, s3, r3, s4, r4, s5, r5, s6, r6) = rest
    p, t = lax.axis_index(POS), lax.axis_index(TILE)
    x, z = p // 4, lax.rem(p, 4)
    y = t // 2
    core, inner, partner = chip_side()
    yz = y * 4 + z
    yes = p >= 0
    x_peers = [(lax.rem(x + k, 4) * 4 + z, t) for k in range(1, 4)]
    x_ids = [lax.rem(x + k, 4) for k in range(1, 4)]
    yz_ids = [lax.rem(yz + k, 16) for k in range(1, 16)]
    yz_peers = [(x * 4 + lax.rem(i, 4), (i // 4) * 2 + core) for i in yz_ids]
    sides = [neighbour(0, -1), neighbour(0, 1)]
    outer, outer_in = neighbour(-inner, 0)
    corners = [neighbour(-inner, -1), neighbour(-inner, 1)]

    load_total = pltpu.make_async_copy(term_ref, total, load_sem.at[0])
    load_own = pltpu.make_async_copy(acc_ref.at[:, pl.ds(1, 4), pl.ds(RIM, 2 * RIM), :], own, load_sem.at[1])
    load_sides = [pltpu.make_async_copy(acc_ref.at[:, b, pl.ds(RIM, 2 * RIM), :], side.at[k], load_sem.at[2 + k])
                  for k, b in enumerate((0, 5))]
    load_total.start()
    for load in load_sides:
        load.start()
    load_own.start()
    greet([(partner, yes), (outer, outer_in)] + sides + corners + [(d, yes) for d in x_peers] + [(d, yes) for d in yz_peers])
    load_total.wait()
    half = 512
    mine = pl.multiple_of(core * half, half)
    other = pl.multiple_of((1 - core) * half, half)
    quarter = half // 4
    order = x_ids + [x]
    firsts = [remote(total.at[pl.ds(pl.multiple_of(other + i * quarter, quarter), quarter)], part1.at[k], s1.at[k], r1.at[k], partner)
              for k, i in enumerate(order)]
    for c in firsts:
        c.start()
    inner_halo = pl.multiple_of((1 - core) * 3 * RIM, RIM)
    outer_halo = pl.multiple_of(core * 3 * RIM, RIM)
    count = 0

    def link(src, dst, device):
        nonlocal count
        copy = remote(src, dst, send_sem.at[count], recv_sem.at[count], device)
        count += 1
        return copy

    inner_corners = [link(acc_ref.at[:, b, pl.ds(inner_halo, RIM), :], recv_c.at[k], partner) for k, b in enumerate((0, 5))]
    for copy in inner_corners:
        copy.start()
    inner_main = link(acc_ref.at[:, pl.ds(1, 4), pl.ds(inner_halo, RIM), :], recv_in, partner)
    outer_main = link(acc_ref.at[:, pl.ds(1, 4), pl.ds(outer_halo, RIM), :], recv_v, outer)
    diagonal = [link(acc_ref.at[:, b, pl.ds(outer_halo, RIM), :], recv_d.at[k], corners[k][0]) for k, b in enumerate((0, 5))]
    across = [link(side.at[k], recv_h.at[k], sides[k][0]) for k in range(2)]
    when_each(outer_in, outer_main.start)
    seconds = []
    for k, i in enumerate(order):
        firsts[k].wait_recv()
        rows = pl.ds(pl.multiple_of(mine + i * quarter, quarter), quarter)
        total[rows] = total[rows] + part1[k]
        if k < 3:
            seconds.append(remote(total.at[rows], part2.at[k], s2.at[k], r2.at[k], x_peers[k]))
            seconds[k].start()
    inner_main.start()
    near = pl.multiple_of((1 - core) * RIM, RIM)
    for k in range(2):
        inner_corners[k].wait()
        load_sides[k].wait()
        side[k, :, pl.ds(near, RIM), :] = side[k, :, pl.ds(near, RIM), :] + recv_c[k]
        when_each(sides[k][1], across[k].start)
    at2 = pl.multiple_of(mine + x * quarter, quarter)
    for c in seconds:
        c.wait_recv()
    total[pl.ds(at2, quarter)] = total[pl.ds(at2, quarter)] + part2[0] + part2[1] + part2[2]
    piece = quarter // 16
    thirds = [remote(total.at[pl.ds(pl.multiple_of(at2 + i * piece, piece), piece)], part3.at[k], s3.at[k], r3.at[k], d)
              for k, (i, d) in enumerate(zip(yz_ids, yz_peers))]
    for c in thirds:
        c.start()
    load_own.wait()
    far = pl.multiple_of(core * RIM, RIM)
    inner_main.wait()

    def add_rows(src, at):
        def body(i, carry):
            plane, b = i // 4, lax.rem(i, 4)
            own[plane, b, pl.ds(at, RIM), :] = own[plane, b, pl.ds(at, RIM), :] + src[plane, b]
            return carry
        lax.fori_loop(0, 8, body, 0)

    add_rows(recv_in, near)
    for c in thirds:
        c.wait_recv()
    at3 = pl.multiple_of(at2 + yz * piece, piece)
    value = total[pl.ds(at3, piece)]
    for k in range(15):
        value = value + part3[k]
    result[pl.ds(at3, piece)] = value * (1.0 / math.sqrt(2048))
    here = result.at[pl.ds(at3, piece)]
    fourths = [remote(here, here, s4.at[k], r4.at[k], d) for k, d in enumerate(yz_peers)]
    for c in fourths:
        c.start()

    @pl.when(outer_in)
    def _():
        outer_main.wait()
        add_rows(recv_v, far)

    for c in fourths:
        c.wait_recv()
    here2 = result.at[pl.ds(at2, quarter)]
    fifths = [remote(here2, here2, s5.at[k], r5.at[k], d) for k, d in enumerate(x_peers)]
    for c in fifths:
        c.start()
    lasts = [remote(here2, here2, s6.at[3], r6.at[3], partner)]
    lasts[0].start()
    for k in range(2):
        when_each(corners[k][1], diagonal[k].start)
    for k in range(2):
        block = 3 - 3 * k
        source, diagonal_source = sides[1 - k][1], corners[1 - k][1]

        @pl.when(source)
        def _():
            across[k].wait_recv()
            own[:, block] = own[:, block] + recv_h[k]

        @pl.when(diagonal_source)
        def _():
            diagonal[k].wait_recv()
            own[:, block, pl.ds(far, RIM), :] = own[:, block, pl.ds(far, RIM), :] + recv_d[k]
    for k, c in enumerate(fifths):
        c.wait_recv()
        from_x = lax.rem(x + 3 - k, 4)
        here1 = result.at[pl.ds(pl.multiple_of(mine + from_x * quarter, quarter), quarter)]
        lasts.append(remote(here1, here1, s6.at[k], r6.at[k], partner))
        lasts[-1].start()
    for c in lasts:
        c.wait_recv()
    for c in firsts + seconds + thirds + fourths + fifths + lasts:
        c.wait_send()
    for k in range(2):
        when_each(sides[k][1], across[k].wait_send)
        when_each(corners[k][1], diagonal[k].wait_send)


def collect(acc, term):
    dma = pltpu.SemaphoreType.DMA
    vmem = lambda *shape: pltpu.VMEM(shape, F32)
    return pl.pallas_call(
        gather_kernel,
        in_specs=[pl.BlockSpec(memory_space=pl.ANY)] * 2,
        out_specs=[pl.BlockSpec(memory_space=pltpu.VMEM)] * 2,
        out_shape=[jax.ShapeDtypeStruct((2, 4, 2 * RIM, LANES), F32), jax.ShapeDtypeStruct((1024, LANES), F32)],
        scratch_shapes=[
            vmem(1024, LANES),
            vmem(2, 4, RIM, LANES), vmem(2, 4, RIM, LANES), vmem(2, 2, RIM, LANES), vmem(2, 2, 2 * RIM, LANES),
            vmem(2, 2, RIM, LANES), vmem(2, 2, 2 * RIM, LANES),
            vmem(4, 128, LANES), vmem(3, 128, LANES), vmem(15, 8, LANES),
            dma((4,)), dma((8,)), dma((8,)), dma((4,)), dma((4,)), dma((3,)), dma((3,)), dma((15,)), dma((15,)),
            dma((15,)), dma((15,)), dma((3,)), dma((3,)), dma((4,)), dma((4,)),
        ],
        compiler_params=pltpu.CompilerParams(collective_id=1, has_side_effects=True, vmem_limit_bytes=16 * 2**20),
        name="collect",
    )(acc, term.reshape(1024, LANES))


def layout_kernel(own_ref, sum_ref, obj_ref, probe_ref, sem):
    copies = [pltpu.make_async_copy(own_ref.at[:, b], obj_ref.at[:, :, pl.ds(b * LANES, LANES)], sem.at[b]) for b in range(4)]
    copies += [pltpu.make_async_copy(sum_ref.at[i // 2, i % 2], probe_ref.at[i // 2, :, pl.ds((i % 2) * LANES, LANES)], sem.at[4 + i])
               for i in range(4)]
    for copy in copies:
        copy.start()
    for copy in copies:
        copy.wait()


def laid_out(own, probe_sum):
    return pl.pallas_call(
        layout_kernel,
        in_specs=[pl.BlockSpec(memory_space=pltpu.VMEM)] * 2,
        out_specs=[pl.BlockSpec(memory_space=pl.ANY)] * 2,
        out_shape=[jax.ShapeDtypeStruct((2, 2 * RIM, 4 * LANES), F32), jax.ShapeDtypeStruct((2, 2 * RIM, 2 * LANES), F32)],
        scratch_shapes=[pltpu.SemaphoreType.DMA((8,))],
        compiler_params=pltpu.CompilerParams(vmem_limit_bytes=4 * 2**20),
        name="layout",
    )(own, probe_sum.reshape(2, 2, 2 * RIM, LANES))


def on_device(object_field, probe_field, measured, offsets):
    fixed = [pltpu.with_memory_space_constraint(a, pltpu.HBM) for a in (object_field, measured, probe_field)]
    ext, ordered, probe = exchange(*fixed)
    acc, term = compute(offsets.T, ext, probe, ordered, jnp.asarray(dft_tables(256)), jnp.asarray(row_tables(256)))
    return tuple(laid_out(*collect(acc, term)))


def solution(mesh):
    placed = (P(None, "tile", "pos"), P(), P(("pos", "tile"), None, None), P(("pos", "tile"), None))
    return jax.shard_map(
        on_device,
        mesh=mesh,
        in_specs=placed,
        out_specs=(P(None, "tile", "pos"), P()),
        check_vma=False,
    )
```

```python
import functools
import math

import jax
import jax.numpy as jnp
import numpy as np
from jax import lax
from jax.experimental import pallas as pl
from jax.experimental.pallas import tpu as pltpu
from jax.sharding import PartitionSpec as P

LANES = 128
RIM = 128
F32 = jnp.float32
BF16 = jnp.bfloat16
MESH = pl.DeviceIdType.MESH


def dft_tables(size):
    half = size // 2
    n = np.arange(half)[:, None]
    k = np.arange(half)[None, :]
    out = []
    for parity in range(2):
        phase = (n * (2 * k + parity)) % size
        table = np.exp(-2j * np.pi * phase / size) / math.sqrt(size)
        real = np.block([[table.real, table.imag], [-table.imag, table.real]])
        out += [real, real.T]
    stack = np.stack(out)
    high = stack.astype(np.float32).astype(BF16)
    low = (stack - high.astype(np.float64)).astype(np.float32).astype(BF16)
    return np.stack([high, low], axis=1)


def row_tables(size):
    quarter = size // 4
    n = np.arange(quarter)[:, None]
    k = np.arange(quarter)[None, :]
    out = []
    for residue in range(4):
        phase = (n * (4 * k + residue)) % size
        table = np.exp(-2j * np.pi * phase / size) / math.sqrt(size)
        real = np.block([[table.real, table.imag], [-table.imag, table.real]])
        out.append([real.T, real])
    stack = np.array(out).transpose(1, 0, 2, 3)
    high = stack.astype(np.float32).astype(BF16)
    low = (stack - high.astype(np.float64)).astype(np.float32).astype(BF16)
    both = np.concatenate([high, high], axis=-1)
    return np.concatenate([both, np.concatenate([low, np.zeros_like(low)], axis=-1)], axis=2)


def split(value):
    high = value.astype(BF16)
    return high, (value - high.astype(F32)).astype(BF16)


def dot(a, b):
    return jnp.dot(a, b, preferred_element_type=F32)


def cat(parts, axis):
    return tuple(jnp.concatenate(p, axis=axis) for p in zip(*parts))


def one_position(chunk, row, col, meas, ext_ref, probe_ref, tab_ref, rtab_ref, acc_ref, term_ref, rolled):
    size, half = 256, 128
    lane = lax.broadcasted_iota(jnp.int32, (chunk, LANES), 1)
    block = col // LANES
    shift = lax.rem(col, LANES)
    mask = lane >= shift

    def patch(start):
        rows = pl.ds(row + start, chunk)
        out = []
        for plane in range(2):
            b0 = ext_ref[plane, block, rows, :]
            b1 = ext_ref[plane, block + 1, rows, :]
            b2 = ext_ref[plane, block + 2, rows, :]
            out.append((jnp.where(mask, b0, b2), b1))
        return out

    sums, diffs = [], []
    for start in range(0, size, chunk):
        rows = pl.ds(start, chunk)
        (x0r, x1r), (x0i, x1i) = patch(start)
        pr = []
        for plane in range(2):
            r0 = pltpu.roll(probe_ref[plane, 0, rows, :], shift, 1)
            r1 = pltpu.roll(probe_ref[plane, 1, rows, :], shift, 1)
            p0 = jnp.where(mask, r0, r1)
            p1 = jnp.where(mask, r1, r0)
            rolled[plane, 0, rows, :] = p0
            rolled[plane, 1, rows, :] = p1
            pr.append((p0, p1))
        (p0r, p1r), (p0i, p1i) = pr
        e0r = p0r * x0r - p0i * x0i
        e0i = p0r * x0i + p0i * x0r
        e1r = p1r * x1r - p1i * x1i
        e1i = p1r * x1i + p1i * x1r
        sums.append(cat([split(e0r + e1r), split(e0i + e1i)], 1))
        diffs.append(cat([split(e0r - e1r), split(e0i - e1i)], 1))
    a, b = cat(sums, 0), cat(diffs, 0)

    def right(data, index):
        t = tab_ref[index, 0]
        return dot(data[0], t) + dot(data[1], t) + dot(data[0], tab_ref[index, 1])

    def left(inverse, residue, stacked):
        product = dot(rtab_ref[inverse, residue], stacked)
        return product[:size // 2] + product[size // 2:]

    def stack(real, imag):
        (rh, rl), (ih, il) = split(real), split(imag)
        return jnp.concatenate([rh, ih, rl, il], axis=0)

    yield
    ye = right(a, 0)
    yo = right(b, 2)
    yield
    quarter = size // 4

    def both(part, m):
        rows = slice(m * quarter, (m + 1) * quarter)
        cols = slice(part * LANES, (part + 1) * LANES)
        return jnp.concatenate([ye[rows, cols], yo[rows, cols]], axis=1)

    re, im = [[both(part, m) for m in range(4)] for part in range(2)]
    t0, t1, t2, t3 = [(re[0] + re[2], im[0] + im[2]), (re[0] - re[2], im[0] - im[2]),
                      (re[1] + re[3], im[1] + im[3]), (re[1] - re[3], im[1] - im[3])]
    inputs = [stack(t0[0] + t2[0], t0[1] + t2[1]), stack(t1[0] + t3[1], t1[1] - t3[0]),
              stack(t0[0] - t2[0], t0[1] - t2[1]), stack(t1[0] - t3[1], t1[1] + t3[0])]
    yield
    waves = [left(0, q, inputs[q]) for q in range(4)]
    yield
    inputs = []
    for q, z in enumerate(waves):
        zr, zi = z[:quarter], z[quarter:]
        power = zr * zr + zi * zi
        factor = 1.0 - meas[pl.ds(q * quarter, quarter), :] * lax.rsqrt(jnp.maximum(power, 1.0))
        inputs.append(stack(zr * factor, zi * factor))
    yield
    v = [left(1, q, inputs[q]) for q in range(4)]
    v = [(w[:quarter], w[quarter:]) for w in v]
    yield
    (s0r, s1r, s2r, s3r), (s0i, s1i, s2i, s3i) = [
        (v[0][c] + v[2][c], v[0][c] - v[2][c], v[1][c] + v[3][c], v[1][c] - v[3][c]) for c in range(2)]
    outs = [(s0r + s2r, s0i + s2i), (s1r - s3i, s1i + s3r), (s0r - s2r, s0i - s2i), (s1r + s3i, s1i - s3r)]
    a, b = [cat([cat([split(xr[:, cols]), split(xi[:, cols])], 1) for xr, xi in outs], 0)
            for cols in (slice(0, LANES), slice(LANES, 2 * LANES))]
    yield
    e = right(a, 1)
    o = right(b, 3)
    yield
    back_shift = lax.rem(LANES - shift, LANES)
    keep = lane < LANES - shift
    for start in range(0, size, chunk):
        rows = pl.ds(start, chunk)
        ee, oo = e[start:start + chunk], o[start:start + chunk]
        b0, b1 = ee + oo, ee - oo
        b0r, b0i = b0[:, :LANES], b0[:, LANES:]
        b1r, b1i = b1[:, :LANES], b1[:, LANES:]
        p0r, p1r = rolled[0, 0, rows, :], rolled[0, 1, rows, :]
        p0i, p1i = rolled[1, 0, rows, :], rolled[1, 1, rows, :]
        grads = ((p0r * b0r + p0i * b0i, p1r * b1r + p1i * b1i),
                 (p0r * b0i - p0i * b0r, p1r * b1i - p1i * b1r))
        (x0r, x1r), (x0i, x1i) = patch(start)
        dst = pl.ds(row + start, chunk)
        for plane, (g0, g1) in enumerate(grads):
            acc_ref[plane, block, dst, :] += jnp.where(mask, g0, 0.0)
            acc_ref[plane, block + 1, dst, :] += g1
            acc_ref[plane, block + 2, dst, :] += jnp.where(mask, 0.0, g0)
        terms = ((x0r * b0r + x0i * b0i, x1r * b1r + x1i * b1i),
                 (x0r * b0i - x0i * b0r, x1r * b1i - x1i * b1r))
        for plane, (t0, t1) in enumerate(terms):
            r0 = pltpu.roll(t0, back_shift, 1)
            r1 = pltpu.roll(t1, back_shift, 1)
            term_ref[plane, 0, rows, :] += jnp.where(keep, r0, r1)
            term_ref[plane, 1, rows, :] += jnp.where(keep, r1, r0)


def compute_kernel(per_step, chunk, off_ref, ext_ref, probe_ref, meas_ref, tab_ref, rtab_ref, acc_ref, term_ref, rolled):
    acc_ref[...] = jnp.zeros_like(acc_ref)
    term_ref[...] = jnp.zeros_like(term_ref)
    stages = 9

    def step(index, carry):
        live = []
        for slot in range(per_step):
            pos = index * per_step + slot
            row = lax.rem(off_ref[0, pos] + 128, 256)
            col = lax.rem(off_ref[1, pos] + 128, 512)
            live.append(one_position(chunk, row, col, meas_ref.at[pos], ext_ref, probe_ref, tab_ref, rtab_ref,
                                     acc_ref, term_ref, rolled.at[slot]))
        for tick in range(stages + per_step - 1):
            for slot, gen in enumerate(live):
                if 0 <= tick - slot < stages:
                    next(gen, None)
        return carry

    lax.fori_loop(0, meas_ref.shape[0] // per_step, step, 0)


def compute(offsets, ext, probe, meas, tables, rows, per_step=4, chunk=32):
    vmem = pl.BlockSpec(memory_space=pltpu.VMEM)
    return pl.pallas_call(
        functools.partial(compute_kernel, per_step, chunk),
        in_specs=[pl.BlockSpec(memory_space=pltpu.SMEM)] + [vmem] * 5,
        out_specs=[vmem] * 2,
        out_shape=[jax.ShapeDtypeStruct(ext.shape, F32), jax.ShapeDtypeStruct(probe.shape, F32)],
        scratch_shapes=[pltpu.VMEM((per_step, 2, 2, 256, 128), F32)],
        compiler_params=pltpu.CompilerParams(vmem_limit_bytes=32 * 2**20),
        name="updates",
    )(offsets, ext, probe, meas, tables, rows)


POS, TILE = "pos", "tile"


def neighbour(dy, dx):
    p, t = lax.axis_index(POS), lax.axis_index(TILE)
    tp, tt = p + dx, t + dy
    inside = (tp >= 0) & (tp < lax.axis_size(POS)) & (tt >= 0) & (tt < lax.axis_size(TILE))
    return (tp, tt), inside


def greet(peers):
    barrier = pltpu.get_barrier_semaphore()
    for device, inside in peers:
        @pl.when(inside)
        def _():
            pl.semaphore_signal(barrier, inc=1, device_id=device, device_id_type=MESH)
    pl.semaphore_wait(barrier, sum(inside.astype(jnp.int32) for _, inside in peers))


def chip_side():
    core = lax.rem(lax.axis_index(TILE), 2)
    inner = 1 - 2 * core
    return core, inner, (lax.axis_index(POS), lax.axis_index(TILE) + inner)


def remote(src, dst, send, recv, device):
    return pltpu.make_async_remote_copy(src_ref=src, dst_ref=dst, send_sem=send, recv_sem=recv,
                                        device_id=device, device_id_type=MESH)


def when_each(condition, *calls):
    @pl.when(condition)
    def _():
        for call in calls:
            call()


def order_table(rows_first, size):
    out = lax.broadcasted_iota(jnp.int32, (size, size), 0 if rows_first else 1)
    src = lax.broadcasted_iota(jnp.int32, (size, size), 1 if rows_first else 0)
    radix = 4 if rows_first else 2
    wanted = lax.rem(out, size // radix) * radix + out // (size // radix)
    return jnp.where(src == wanted, 1.0, 0.0).astype(BF16)


def halo_kernel(obj_ref, meas_ref, prb_ref, ext_ref, out_ref, probe_ref, zeros, loaded, ordered, send_sem, recv_sem,
                fill_sem, own_sem, in_sem, out_sem, relay_send, relay_recv, probe_sem):
    group = loaded.shape[0] // in_sem.shape[0]
    size = loaded.shape[1]
    core, inner, partner = chip_side()
    p, t = lax.axis_index(POS), lax.axis_index(TILE)
    loads = [pltpu.make_async_copy(meas_ref.at[pl.ds(g * group, group)], loaded.at[pl.ds(g * group, group)], in_sem.at[g])
             for g in range(in_sem.shape[0])]
    locals_ = [pltpu.make_async_copy(obj_ref.at[:, :, pl.ds(b * LANES, LANES)], ext_ref.at[:, b + 1, pl.ds(RIM, 2 * RIM), :],
                                     own_sem.at[b]) for b in range(4)]
    locals_ += [pltpu.make_async_copy(prb_ref.at[:, :, pl.ds(b * LANES, LANES)], probe_ref.at[:, b], probe_sem.at[b])
                for b in range(2)]
    sides = [neighbour(0, -1), neighbour(0, 1)]
    outer, outer_in = neighbour(-inner, 0)
    for load in loads:
        load.start()
    greet(sides + [(outer, outer_in), (partner, p >= 0)])
    inner_row = pl.multiple_of((1 - core) * RIM, RIM)
    outer_row = pl.multiple_of(core * RIM, RIM)
    inner_halo = pl.multiple_of((1 - core) * 3 * RIM, RIM)
    outer_halo = pl.multiple_of(core * 3 * RIM, RIM)
    pairs = []

    def add(src_row, count, block, dst_block, dst_row, device, there, source_there, fill_row):
        index = len(pairs)
        copy = remote(obj_ref.at[:, pl.ds(src_row, count), pl.ds(block * LANES, LANES)],
                      ext_ref.at[:, dst_block, pl.ds(dst_row, count), :], send_sem.at[index], recv_sem.at[index], device)
        fill = pltpu.make_async_copy(zeros.at[:, pl.ds(0, count), :], ext_ref.at[:, dst_block, pl.ds(fill_row, count), :],
                                     fill_sem.at[index])
        pairs.append((copy, there, source_there, fill))
        when_each(there, copy.start)

    inner_own = pl.multiple_of((2 - core) * RIM, RIM)
    outer_own = pl.multiple_of((1 + core) * RIM, RIM)
    there_row = pl.multiple_of((1 - core) * 3 * RIM, RIM)

    def add_sides(row, own_row):
        add(row, RIM, 0, 5, own_row, sides[0][0], sides[0][1], sides[1][1], own_row)
        add(row, RIM, 3, 0, own_row, sides[1][0], sides[1][1], sides[0][1], own_row)

    add_sides(outer_row, outer_own)
    for b in range(4):
        add(outer_row, RIM, b, b + 1, there_row, outer, outer_in, outer_in, outer_halo)
    add_sides(inner_row, inner_own)
    partner_halo = pl.multiple_of(core * 3 * RIM, RIM)
    inside = [remote(obj_ref.at[:, pl.ds(inner_row, RIM), pl.ds(b * LANES, LANES)],
                     ext_ref.at[:, b + 1, pl.ds(partner_halo, RIM), :], relay_send.at[b], relay_recv.at[b], partner)
              for b in range(4)]
    for copy in inside:
        copy.start()
    for copy in locals_:
        copy.start()
    zeros[...] = jnp.zeros_like(zeros)
    for copy, there, source_there, fill in pairs:
        when_each(jnp.logical_not(source_there), fill.start)
    perm_rows, perm_cols = order_table(True, size), order_table(False, size)
    stores = []

    def side_landed(k):
        copy, _, source_there, fill = pairs[k]
        when_each(source_there, copy.wait_recv)
        when_each(jnp.logical_not(source_there), fill.wait)

    edge, edge_fill = [], []

    def relay_edge():
        for k, block in enumerate((5, 0)):
            side_landed(k)
            edge.append(remote(ext_ref.at[:, block, pl.ds(outer_own, RIM), :], ext_ref.at[:, block, pl.ds(there_row, RIM), :],
                               relay_send.at[6 + k], relay_recv.at[6 + k], outer))
            edge_fill.append(pltpu.make_async_copy(zeros, ext_ref.at[:, block, pl.ds(outer_halo, RIM), :], fill_sem.at[8 + k]))
            when_each(outer_in, edge[k].start)
            when_each(jnp.logical_not(outer_in), edge_fill[k].start)

    def relay_inner():
        for k, block in enumerate((5, 0)):
            side_landed(6 + k)
            inside.append(remote(ext_ref.at[:, block, pl.ds(inner_own, RIM), :], ext_ref.at[:, block, pl.ds(partner_halo, RIM), :],
                                 relay_send.at[4 + k], relay_recv.at[4 + k], partner))
            inside[-1].start()

    for g in range(in_sem.shape[0]):
        loads[g].wait()

        def order(i, carry):
            at = g * group + 2 * i
            parts = [split(loaded[at + j]) for j in range(2)]
            done = None
            for k in range(2):
                rows = jnp.concatenate([parts[0][k], parts[1][k]], axis=0)
                moved = dot(rows, perm_cols).astype(BF16)
                moved = jnp.concatenate([moved[:size], moved[size:]], axis=1)
                moved = dot(perm_rows, moved)
                done = moved if done is None else done + moved
            ordered[at] = done[:, :size]
            ordered[at + 1] = done[:, size:]
            return carry

        lax.fori_loop(0, group // 2, order, 0)
        store = pltpu.make_async_copy(ordered.at[pl.ds(g * group, group)], out_ref.at[pl.ds(g * group, group)], out_sem.at[g])
        store.start()
        stores.append(store)
        if g == in_sem.shape[0] - 2:
            relay_edge()
    relay_inner()
    for copy in stores + locals_:
        copy.wait()
    for index, (copy, there, source_there, fill) in enumerate(pairs):
        when_each(there, copy.wait_send)
        if 2 <= index < 6:
            side_landed(index)
    for copy in inside:
        copy.wait()
    for k in range(2):
        when_each(outer_in, edge[k].wait)
        when_each(jnp.logical_not(outer_in), edge_fill[k].wait)


def exchange(object_field, measured, probe_field):
    groups = 4
    dma = pltpu.SemaphoreType.DMA
    anywhere = pl.BlockSpec(memory_space=pl.ANY)
    return pl.pallas_call(
        halo_kernel,
        in_specs=[pl.BlockSpec(memory_space=pltpu.HBM)] * 3,
        out_specs=[anywhere] * 3,
        out_shape=[jax.ShapeDtypeStruct((2, 6, 4 * RIM, LANES), F32), jax.ShapeDtypeStruct(measured.shape, F32),
                   jax.ShapeDtypeStruct((2, 2, 2 * RIM, LANES), F32)],
        scratch_shapes=[
            pltpu.VMEM((2, RIM, LANES), F32),
            pltpu.VMEM(measured.shape, F32),
            pltpu.VMEM(measured.shape, F32),
            dma((8,)), dma((8,)), dma((10,)),
            dma((4,)), dma((groups,)), dma((groups,)), dma((8,)), dma((8,)), dma((2,)),
        ],
        compiler_params=pltpu.CompilerParams(collective_id=0, has_side_effects=True, vmem_limit_bytes=16 * 2**20),
        name="halo",
    )(object_field, measured, probe_field)


def gather_kernel(acc_ref, term_ref, own, result, total, *rest):
    (recv_v, recv_in, recv_c, recv_h, recv_d, side, part1, part2, part3,
     load_sem, send_sem, recv_sem, s1, r1, s2, r2, s3, r3, s4, r4, s5, r5, s6, r6) = rest
    p, t = lax.axis_index(POS), lax.axis_index(TILE)
    x, z = p // 4, lax.rem(p, 4)
    y = t // 2
    core, inner, partner = chip_side()
    yz = y * 4 + z
    yes = p >= 0
    x_peers = [(lax.rem(x + k, 4) * 4 + z, t) for k in range(1, 4)]
    x_ids = [lax.rem(x + k, 4) for k in range(1, 4)]
    yz_ids = [lax.rem(yz + k, 16) for k in range(1, 16)]
    yz_peers = [(x * 4 + lax.rem(i, 4), (i // 4) * 2 + core) for i in yz_ids]
    sides = [neighbour(0, -1), neighbour(0, 1)]
    outer, outer_in = neighbour(-inner, 0)
    corners = [neighbour(-inner, -1), neighbour(-inner, 1)]

    load_total = pltpu.make_async_copy(term_ref, total, load_sem.at[0])
    load_own = pltpu.make_async_copy(acc_ref.at[:, pl.ds(1, 4), pl.ds(RIM, 2 * RIM), :], own, load_sem.at[1])
    load_sides = [pltpu.make_async_copy(acc_ref.at[:, b, pl.ds(RIM, 2 * RIM), :], side.at[k], load_sem.at[2 + k])
                  for k, b in enumerate((0, 5))]
    load_total.start()
    for load in load_sides:
        load.start()
    load_own.start()
    greet([(partner, yes), (outer, outer_in)] + sides + corners + [(d, yes) for d in x_peers] + [(d, yes) for d in yz_peers])
    load_total.wait()
    half = 512
    mine = pl.multiple_of(core * half, half)
    other = pl.multiple_of((1 - core) * half, half)
    quarter = half // 4
    order = x_ids + [x]
    firsts = [remote(total.at[pl.ds(pl.multiple_of(other + i * quarter, quarter), quarter)], part1.at[k], s1.at[k], r1.at[k], partner)
              for k, i in enumerate(order)]
    for c in firsts:
        c.start()
    inner_halo = pl.multiple_of((1 - core) * 3 * RIM, RIM)
    outer_halo = pl.multiple_of(core * 3 * RIM, RIM)
    count = 0

    def link(src, dst, device):
        nonlocal count
        copy = remote(src, dst, send_sem.at[count], recv_sem.at[count], device)
        count += 1
        return copy

    inner_corners = [link(acc_ref.at[:, b, pl.ds(inner_halo, RIM), :], recv_c.at[k], partner) for k, b in enumerate((0, 5))]
    for copy in inner_corners:
        copy.start()
    inner_main = link(acc_ref.at[:, pl.ds(1, 4), pl.ds(inner_halo, RIM), :], recv_in, partner)
    outer_main = link(acc_ref.at[:, pl.ds(1, 4), pl.ds(outer_halo, RIM), :], recv_v, outer)
    diagonal = [link(acc_ref.at[:, b, pl.ds(outer_halo, RIM), :], recv_d.at[k], corners[k][0]) for k, b in enumerate((0, 5))]
    across = [link(side.at[k], recv_h.at[k], sides[k][0]) for k in range(2)]
    when_each(outer_in, outer_main.start)
    seconds = []
    for k, i in enumerate(order):
        firsts[k].wait_recv()
        rows = pl.ds(pl.multiple_of(mine + i * quarter, quarter), quarter)
        total[rows] = total[rows] + part1[k]
        if k < 3:
            seconds.append(remote(total.at[rows], part2.at[k], s2.at[k], r2.at[k], x_peers[k]))
            seconds[k].start()
    inner_main.start()
    near = pl.multiple_of((1 - core) * RIM, RIM)
    for k in range(2):
        inner_corners[k].wait()
        load_sides[k].wait()
        side[k, :, pl.ds(near, RIM), :] = side[k, :, pl.ds(near, RIM), :] + recv_c[k]
        when_each(sides[k][1], across[k].start)
    at2 = pl.multiple_of(mine + x * quarter, quarter)
    for c in seconds:
        c.wait_recv()
    total[pl.ds(at2, quarter)] = total[pl.ds(at2, quarter)] + part2[0] + part2[1] + part2[2]
    piece = quarter // 16
    thirds = [remote(total.at[pl.ds(pl.multiple_of(at2 + i * piece, piece), piece)], part3.at[k], s3.at[k], r3.at[k], d)
              for k, (i, d) in enumerate(zip(yz_ids, yz_peers))]
    for c in thirds:
        c.start()
    load_own.wait()
    far = pl.multiple_of(core * RIM, RIM)
    inner_main.wait()

    def add_rows(src, at):
        def body(i, carry):
            plane, b = i // 4, lax.rem(i, 4)
            own[plane, b, pl.ds(at, RIM), :] = own[plane, b, pl.ds(at, RIM), :] + src[plane, b]
            return carry
        lax.fori_loop(0, 8, body, 0)

    add_rows(recv_in, near)
    for c in thirds:
        c.wait_recv()
    at3 = pl.multiple_of(at2 + yz * piece, piece)
    value = total[pl.ds(at3, piece)]
    for k in range(15):
        value = value + part3[k]
    result[pl.ds(at3, piece)] = value * (1.0 / math.sqrt(2048))
    here = result.at[pl.ds(at3, piece)]
    fourths = [remote(here, here, s4.at[k], r4.at[k], d) for k, d in enumerate(yz_peers)]
    for c in fourths:
        c.start()

    @pl.when(outer_in)
    def _():
        outer_main.wait()
        add_rows(recv_v, far)

    for c in fourths:
        c.wait_recv()
    here2 = result.at[pl.ds(at2, quarter)]
    fifths = [remote(here2, here2, s5.at[k], r5.at[k], d) for k, d in enumerate(x_peers)]
    for c in fifths:
        c.start()
    lasts = [remote(here2, here2, s6.at[3], r6.at[3], partner)]
    lasts[0].start()
    for k in range(2):
        when_each(corners[k][1], diagonal[k].start)
    for k in range(2):
        block = 3 - 3 * k
        source, diagonal_source = sides[1 - k][1], corners[1 - k][1]

        @pl.when(source)
        def _():
            across[k].wait_recv()
            own[:, block] = own[:, block] + recv_h[k]

        @pl.when(diagonal_source)
        def _():
            diagonal[k].wait_recv()
            own[:, block, pl.ds(far, RIM), :] = own[:, block, pl.ds(far, RIM), :] + recv_d[k]
    for k, c in enumerate(fifths):
        c.wait_recv()
        from_x = lax.rem(x + 3 - k, 4)
        here1 = result.at[pl.ds(pl.multiple_of(mine + from_x * quarter, quarter), quarter)]
        lasts.append(remote(here1, here1, s6.at[k], r6.at[k], partner))
        lasts[-1].start()
    for c in lasts:
        c.wait_recv()
    for c in firsts + seconds + thirds + fourths + fifths + lasts:
        c.wait_send()
    for k in range(2):
        when_each(sides[k][1], across[k].wait_send)
        when_each(corners[k][1], diagonal[k].wait_send)


def collect(acc, term):
    dma = pltpu.SemaphoreType.DMA
    vmem = lambda *shape: pltpu.VMEM(shape, F32)
    return pl.pallas_call(
        gather_kernel,
        in_specs=[pl.BlockSpec(memory_space=pl.ANY)] * 2,
        out_specs=[pl.BlockSpec(memory_space=pltpu.VMEM)] * 2,
        out_shape=[jax.ShapeDtypeStruct((2, 4, 2 * RIM, LANES), F32), jax.ShapeDtypeStruct((1024, LANES), F32)],
        scratch_shapes=[
            vmem(1024, LANES),
            vmem(2, 4, RIM, LANES), vmem(2, 4, RIM, LANES), vmem(2, 2, RIM, LANES), vmem(2, 2, 2 * RIM, LANES),
            vmem(2, 2, RIM, LANES), vmem(2, 2, 2 * RIM, LANES),
            vmem(4, 128, LANES), vmem(3, 128, LANES), vmem(15, 8, LANES),
            dma((4,)), dma((8,)), dma((8,)), dma((4,)), dma((4,)), dma((3,)), dma((3,)), dma((15,)), dma((15,)),
            dma((15,)), dma((15,)), dma((3,)), dma((3,)), dma((4,)), dma((4,)),
        ],
        compiler_params=pltpu.CompilerParams(collective_id=1, has_side_effects=True, vmem_limit_bytes=16 * 2**20),
        name="collect",
    )(acc, term.reshape(1024, LANES))


def layout_kernel(own_ref, sum_ref, obj_ref, probe_ref, sem):
    copies = [pltpu.make_async_copy(own_ref.at[:, b], obj_ref.at[:, :, pl.ds(b * LANES, LANES)], sem.at[b]) for b in range(4)]
    copies += [pltpu.make_async_copy(sum_ref.at[i // 2, i % 2], probe_ref.at[i // 2, :, pl.ds((i % 2) * LANES, LANES)], sem.at[4 + i])
               for i in range(4)]
    for copy in copies:
        copy.start()
    for copy in copies:
        copy.wait()


def laid_out(own, probe_sum):
    return pl.pallas_call(
        layout_kernel,
        in_specs=[pl.BlockSpec(memory_space=pltpu.VMEM)] * 2,
        out_specs=[pl.BlockSpec(memory_space=pl.ANY)] * 2,
        out_shape=[jax.ShapeDtypeStruct((2, 2 * RIM, 4 * LANES), F32), jax.ShapeDtypeStruct((2, 2 * RIM, 2 * LANES), F32)],
        scratch_shapes=[pltpu.SemaphoreType.DMA((8,))],
        compiler_params=pltpu.CompilerParams(vmem_limit_bytes=4 * 2**20),
        name="layout",
    )(own, probe_sum.reshape(2, 2, 2 * RIM, LANES))


def on_device(object_field, probe_field, measured, offsets):
    fixed = [pltpu.with_memory_space_constraint(a, pltpu.HBM) for a in (object_field, measured, probe_field)]
    ext, ordered, probe = exchange(*fixed)
    acc, term = compute(offsets.T, ext, probe, ordered, jnp.asarray(dft_tables(256)), jnp.asarray(row_tables(256)))
    return tuple(laid_out(*collect(acc, term)))


def solution(mesh):
    placed = (P(None, "tile", "pos"), P(), P(("pos", "tile"), None, None), P(("pos", "tile"), None))
    return jax.shard_map(
        on_device,
        mesh=mesh,
        in_specs=placed,
        out_specs=(P(None, "tile", "pos"), P()),
        check_vma=False,
    )
```

```python
import functools
import math

import jax
import jax.numpy as jnp
import numpy as np
from jax import lax
from jax.experimental import pallas as pl
from jax.experimental.pallas import tpu as pltpu
from jax.sharding import PartitionSpec as P

LANES = 128
RIM = 128
F32 = jnp.float32
BF16 = jnp.bfloat16
MESH = pl.DeviceIdType.MESH


def dft_tables(size):
    half = size // 2
    n = np.arange(half)[:, None]
    k = np.arange(half)[None, :]
    out = []
    for parity in range(2):
        phase = (n * (2 * k + parity)) % size
        table = np.exp(-2j * np.pi * phase / size) / math.sqrt(size)
        real = np.block([[table.real, table.imag], [-table.imag, table.real]])
        out += [real, real.T]
    stack = np.stack(out)
    high = stack.astype(np.float32).astype(BF16)
    low = (stack - high.astype(np.float64)).astype(np.float32).astype(BF16)
    return np.stack([high, low], axis=1)


def row_tables(size):
    quarter = size // 4
    n = np.arange(quarter)[:, None]
    k = np.arange(quarter)[None, :]
    out = []
    for residue in range(4):
        phase = (n * (4 * k + residue)) % size
        table = np.exp(-2j * np.pi * phase / size) / math.sqrt(size)
        real = np.block([[table.real, table.imag], [-table.imag, table.real]])
        out.append([real.T, real])
    stack = np.array(out).transpose(1, 0, 2, 3)
    high = stack.astype(np.float32).astype(BF16)
    low = (stack - high.astype(np.float64)).astype(np.float32).astype(BF16)
    both = np.concatenate([high, high], axis=-1)
    return np.concatenate([both, np.concatenate([low, np.zeros_like(low)], axis=-1)], axis=2)


def split(value):
    high = value.astype(BF16)
    return high, (value - high.astype(F32)).astype(BF16)


def dot(a, b):
    return jnp.dot(a, b, preferred_element_type=F32)


def cat(parts, axis):
    return tuple(jnp.concatenate(p, axis=axis) for p in zip(*parts))


def one_position(chunk, row, col, meas, ext_ref, probe_ref, tab_ref, rtab_ref, acc_ref, term_ref, rolled):
    size, half = 256, 128
    lane = lax.broadcasted_iota(jnp.int32, (chunk, LANES), 1)
    block = col // LANES
    shift = lax.rem(col, LANES)
    mask = lane >= shift

    def patch(start):
        rows = pl.ds(row + start, chunk)
        out = []
        for plane in range(2):
            b0 = ext_ref[plane, block, rows, :]
            b1 = ext_ref[plane, block + 1, rows, :]
            b2 = ext_ref[plane, block + 2, rows, :]
            out.append((jnp.where(mask, b0, b2), b1))
        return out

    sums, diffs = [], []
    for start in range(0, size, chunk):
        rows = pl.ds(start, chunk)
        (x0r, x1r), (x0i, x1i) = patch(start)
        pr = []
        for plane in range(2):
            r0 = pltpu.roll(probe_ref[plane, 0, rows, :], shift, 1)
            r1 = pltpu.roll(probe_ref[plane, 1, rows, :], shift, 1)
            p0 = jnp.where(mask, r0, r1)
            p1 = jnp.where(mask, r1, r0)
            rolled[plane, 0, rows, :] = p0
            rolled[plane, 1, rows, :] = p1
            pr.append((p0, p1))
        (p0r, p1r), (p0i, p1i) = pr
        e0r = p0r * x0r - p0i * x0i
        e0i = p0r * x0i + p0i * x0r
        e1r = p1r * x1r - p1i * x1i
        e1i = p1r * x1i + p1i * x1r
        if start + chunk == size // 2:
            yield
        sums.append(cat([split(e0r + e1r), split(e0i + e1i)], 1))
        diffs.append(cat([split(e0r - e1r), split(e0i - e1i)], 1))
    a, b = cat(sums, 0), cat(diffs, 0)

    def right(data, index):
        t = tab_ref[index, 0]
        return dot(data[0], t) + dot(data[1], t) + dot(data[0], tab_ref[index, 1])

    def left(inverse, residue, stacked):
        product = dot(rtab_ref[inverse, residue], stacked)
        return product[:size // 2] + product[size // 2:]

    def stack(real, imag):
        (rh, rl), (ih, il) = split(real), split(imag)
        return jnp.concatenate([rh, ih, rl, il], axis=0)

    yield
    ye = right(a, 0)
    yo = right(b, 2)
    yield
    quarter = size // 4

    def both(part, m):
        rows = slice(m * quarter, (m + 1) * quarter)
        cols = slice(part * LANES, (part + 1) * LANES)
        return jnp.concatenate([ye[rows, cols], yo[rows, cols]], axis=1)

    re, im = [[both(part, m) for m in range(4)] for part in range(2)]
    t0, t1, t2, t3 = [(re[0] + re[2], im[0] + im[2]), (re[0] - re[2], im[0] - im[2]),
                      (re[1] + re[3], im[1] + im[3]), (re[1] - re[3], im[1] - im[3])]
    inputs = [stack(t0[0] + t2[0], t0[1] + t2[1]), stack(t1[0] + t3[1], t1[1] - t3[0]),
              stack(t0[0] - t2[0], t0[1] - t2[1]), stack(t1[0] - t3[1], t1[1] + t3[0])]
    yield
    waves = [left(0, q, inputs[q]) for q in range(4)]
    yield
    inputs = []
    for q, z in enumerate(waves):
        zr, zi = z[:quarter], z[quarter:]
        power = zr * zr + zi * zi
        factor = 1.0 - meas[pl.ds(q * quarter, quarter), :] * lax.rsqrt(jnp.maximum(power, 1.0))
        inputs.append(stack(zr * factor, zi * factor))
    yield
    v = [left(1, q, inputs[q]) for q in range(4)]
    v = [(w[:quarter], w[quarter:]) for w in v]
    yield
    (s0r, s1r, s2r, s3r), (s0i, s1i, s2i, s3i) = [
        (v[0][c] + v[2][c], v[0][c] - v[2][c], v[1][c] + v[3][c], v[1][c] - v[3][c]) for c in range(2)]
    outs = [(s0r + s2r, s0i + s2i), (s1r - s3i, s1i + s3r), (s0r - s2r, s0i - s2i), (s1r + s3i, s1i - s3r)]
    a, b = [cat([cat([split(xr[:, cols]), split(xi[:, cols])], 1) for xr, xi in outs], 0)
            for cols in (slice(0, LANES), slice(LANES, 2 * LANES))]
    yield
    e = right(a, 1)
    o = right(b, 3)
    yield
    back_shift = lax.rem(LANES - shift, LANES)
    keep = lane < LANES - shift
    for start in range(0, size, chunk):
        rows = pl.ds(start, chunk)
        ee, oo = e[start:start + chunk], o[start:start + chunk]
        b0, b1 = ee + oo, ee - oo
        b0r, b0i = b0[:, :LANES], b0[:, LANES:]
        b1r, b1i = b1[:, :LANES], b1[:, LANES:]
        p0r, p1r = rolled[0, 0, rows, :], rolled[0, 1, rows, :]
        p0i, p1i = rolled[1, 0, rows, :], rolled[1, 1, rows, :]
        grads = ((p0r * b0r + p0i * b0i, p1r * b1r + p1i * b1i),
                 (p0r * b0i - p0i * b0r, p1r * b1i - p1i * b1r))
        (x0r, x1r), (x0i, x1i) = patch(start)
        dst = pl.ds(row + start, chunk)
        for plane, (g0, g1) in enumerate(grads):
            acc_ref[plane, block, dst, :] += jnp.where(mask, g0, 0.0)
            acc_ref[plane, block + 1, dst, :] += g1
            acc_ref[plane, block + 2, dst, :] += jnp.where(mask, 0.0, g0)
        terms = ((x0r * b0r + x0i * b0i, x1r * b1r + x1i * b1i),
                 (x0r * b0i - x0i * b0r, x1r * b1i - x1i * b1r))
        for plane, (t0, t1) in enumerate(terms):
            r0 = pltpu.roll(t0, back_shift, 1)
            r1 = pltpu.roll(t1, back_shift, 1)
            term_ref[plane, 0, rows, :] += jnp.where(keep, r0, r1)
            term_ref[plane, 1, rows, :] += jnp.where(keep, r1, r0)
        if start + chunk == size // 2:
            yield


def compute_kernel(per_step, chunk, off_ref, ext_ref, probe_ref, meas_ref, tab_ref, rtab_ref, zero_acc, zero_term, acc_ref, term_ref, rolled):
    stages = 11

    def step(index, carry):
        live = []
        for slot in range(per_step):
            pos = index * per_step + slot
            row = lax.rem(off_ref[0, pos] + 128, 256)
            col = lax.rem(off_ref[1, pos] + 128, 512)
            live.append(one_position(chunk, row, col, meas_ref.at[pos], ext_ref, probe_ref, tab_ref, rtab_ref,
                                     acc_ref, term_ref, rolled.at[slot]))
        for tick in range(stages + per_step - 1):
            for slot, gen in enumerate(live):
                if 0 <= tick - slot < stages:
                    next(gen, None)
        return carry

    lax.fori_loop(0, meas_ref.shape[0] // per_step, step, 0)


def compute(offsets, ext, probe, meas, tables, rows, acc, term, per_step=4, chunk=32):
    vmem = pl.BlockSpec(memory_space=pltpu.VMEM)
    return pl.pallas_call(
        functools.partial(compute_kernel, per_step, chunk),
        in_specs=[pl.BlockSpec(memory_space=pltpu.SMEM)] + [vmem] * 7,
        out_specs=[vmem] * 2,
        out_shape=[jax.ShapeDtypeStruct(ext.shape, F32), jax.ShapeDtypeStruct(probe.shape, F32)],
        scratch_shapes=[pltpu.VMEM((per_step, 2, 2, 256, 128), F32)],
        compiler_params=pltpu.CompilerParams(vmem_limit_bytes=32 * 2**20),
        input_output_aliases={6: 0, 7: 1},
        name="updates",
    )(offsets, ext, probe, meas, tables, rows, acc, term)


POS, TILE = "pos", "tile"


def neighbour(dy, dx):
    p, t = lax.axis_index(POS), lax.axis_index(TILE)
    tp, tt = p + dx, t + dy
    inside = (tp >= 0) & (tp < lax.axis_size(POS)) & (tt >= 0) & (tt < lax.axis_size(TILE))
    return (tp, tt), inside


def greet(peers):
    barrier = pltpu.get_barrier_semaphore()
    for device, inside in peers:
        @pl.when(inside)
        def _():
            pl.semaphore_signal(barrier, inc=1, device_id=device, device_id_type=MESH)
    pl.semaphore_wait(barrier, sum(inside.astype(jnp.int32) for _, inside in peers))


def chip_side():
    core = lax.rem(lax.axis_index(TILE), 2)
    inner = 1 - 2 * core
    return core, inner, (lax.axis_index(POS), lax.axis_index(TILE) + inner)


def remote(src, dst, send, recv, device):
    return pltpu.make_async_remote_copy(src_ref=src, dst_ref=dst, send_sem=send, recv_sem=recv,
                                        device_id=device, device_id_type=MESH)


def when_each(condition, *calls):
    @pl.when(condition)
    def _():
        for call in calls:
            call()


def order_table(rows_first, size):
    out = lax.broadcasted_iota(jnp.int32, (size, size), 0 if rows_first else 1)
    src = lax.broadcasted_iota(jnp.int32, (size, size), 1 if rows_first else 0)
    radix = 4 if rows_first else 2
    wanted = lax.rem(out, size // radix) * radix + out // (size // radix)
    return jnp.where(src == wanted, 1.0, 0.0).astype(BF16)


def halo_kernel(obj_ref, meas_ref, prb_ref, ext_ref, out_ref, probe_ref, acc_ref, term_ref, zeros, loaded, ordered, send_sem, recv_sem,
                fill_sem, own_sem, in_sem, out_sem, relay_send, relay_recv, probe_sem):
    group = loaded.shape[0] // in_sem.shape[0]
    size = loaded.shape[1]
    core, inner, partner = chip_side()
    p, t = lax.axis_index(POS), lax.axis_index(TILE)
    loads = [pltpu.make_async_copy(meas_ref.at[pl.ds(g * group, group)], loaded.at[pl.ds(g * group, group)], in_sem.at[g])
             for g in range(in_sem.shape[0])]
    locals_ = [pltpu.make_async_copy(obj_ref.at[:, :, pl.ds(b * LANES, LANES)], ext_ref.at[:, b + 1, pl.ds(RIM, 2 * RIM), :],
                                     own_sem.at[b]) for b in range(4)]
    locals_ += [pltpu.make_async_copy(prb_ref.at[:, :, pl.ds(b * LANES, LANES)], probe_ref.at[:, b], probe_sem.at[b])
                for b in range(2)]
    sides = [neighbour(0, -1), neighbour(0, 1)]
    outer, outer_in = neighbour(-inner, 0)
    for load in loads:
        load.start()
    greet(sides + [(outer, outer_in), (partner, p >= 0)])
    inner_row = pl.multiple_of((1 - core) * RIM, RIM)
    outer_row = pl.multiple_of(core * RIM, RIM)
    inner_halo = pl.multiple_of((1 - core) * 3 * RIM, RIM)
    outer_halo = pl.multiple_of(core * 3 * RIM, RIM)
    pairs = []

    def add(src_row, count, block, dst_block, dst_row, device, there, source_there, fill_row):
        index = len(pairs)
        copy = remote(obj_ref.at[:, pl.ds(src_row, count), pl.ds(block * LANES, LANES)],
                      ext_ref.at[:, dst_block, pl.ds(dst_row, count), :], send_sem.at[index], recv_sem.at[index], device)
        fill = pltpu.make_async_copy(zeros.at[:, pl.ds(0, count), :], ext_ref.at[:, dst_block, pl.ds(fill_row, count), :],
                                     fill_sem.at[index])
        pairs.append((copy, there, source_there, fill))
        when_each(there, copy.start)

    inner_own = pl.multiple_of((2 - core) * RIM, RIM)
    outer_own = pl.multiple_of((1 + core) * RIM, RIM)
    there_row = pl.multiple_of((1 - core) * 3 * RIM, RIM)

    def add_sides(row, own_row):
        add(row, RIM, 0, 5, own_row, sides[0][0], sides[0][1], sides[1][1], own_row)
        add(row, RIM, 3, 0, own_row, sides[1][0], sides[1][1], sides[0][1], own_row)

    add_sides(outer_row, outer_own)
    for b in range(4):
        add(outer_row, RIM, b, b + 1, there_row, outer, outer_in, outer_in, outer_halo)
    add_sides(inner_row, inner_own)
    partner_halo = pl.multiple_of(core * 3 * RIM, RIM)
    inside = [remote(obj_ref.at[:, pl.ds(inner_row, RIM), pl.ds(b * LANES, LANES)],
                     ext_ref.at[:, b + 1, pl.ds(partner_halo, RIM), :], relay_send.at[b], relay_recv.at[b], partner)
              for b in range(4)]
    for copy in inside:
        copy.start()
    for copy in locals_:
        copy.start()
    zeros[...] = jnp.zeros_like(zeros)
    acc_ref[...] = jnp.zeros_like(acc_ref)
    term_ref[...] = jnp.zeros_like(term_ref)
    for copy, there, source_there, fill in pairs:
        when_each(jnp.logical_not(source_there), fill.start)
    perm_rows, perm_cols = order_table(True, size), order_table(False, size)
    stores = []

    def side_landed(k):
        copy, _, source_there, fill = pairs[k]
        when_each(source_there, copy.wait_recv)
        when_each(jnp.logical_not(source_there), fill.wait)

    edge, edge_fill = [], []

    def relay_edge():
        for k, block in enumerate((5, 0)):
            side_landed(k)
            edge.append(remote(ext_ref.at[:, block, pl.ds(outer_own, RIM), :], ext_ref.at[:, block, pl.ds(there_row, RIM), :],
                               relay_send.at[6 + k], relay_recv.at[6 + k], outer))
            edge_fill.append(pltpu.make_async_copy(zeros, ext_ref.at[:, block, pl.ds(outer_halo, RIM), :], fill_sem.at[8 + k]))
            when_each(outer_in, edge[k].start)
            when_each(jnp.logical_not(outer_in), edge_fill[k].start)

    def relay_inner():
        for k, block in enumerate((5, 0)):
            side_landed(6 + k)
            inside.append(remote(ext_ref.at[:, block, pl.ds(inner_own, RIM), :], ext_ref.at[:, block, pl.ds(partner_halo, RIM), :],
                                 relay_send.at[4 + k], relay_recv.at[4 + k], partner))
            inside[-1].start()

    for g in range(in_sem.shape[0]):
        loads[g].wait()

        def order(i, carry):
            at = g * group + 2 * i
            parts = [split(loaded[at + j]) for j in range(2)]
            done = None
            for k in range(2):
                rows = jnp.concatenate([parts[0][k], parts[1][k]], axis=0)
                moved = dot(rows, perm_cols).astype(BF16)
                moved = jnp.concatenate([moved[:size], moved[size:]], axis=1)
                moved = dot(perm_rows, moved)
                done = moved if done is None else done + moved
            ordered[at] = done[:, :size]
            ordered[at + 1] = done[:, size:]
            return carry

        lax.fori_loop(0, group // 2, order, 0)
        store = pltpu.make_async_copy(ordered.at[pl.ds(g * group, group)], out_ref.at[pl.ds(g * group, group)], out_sem.at[g])
        store.start()
        stores.append(store)
        if g == in_sem.shape[0] - 2:
            relay_edge()
    relay_inner()
    for copy in stores + locals_:
        copy.wait()
    for index, (copy, there, source_there, fill) in enumerate(pairs):
        when_each(there, copy.wait_send)
        if 2 <= index < 6:
            side_landed(index)
    for copy in inside:
        copy.wait()
    for k in range(2):
        when_each(outer_in, edge[k].wait)
        when_each(jnp.logical_not(outer_in), edge_fill[k].wait)


def exchange(object_field, measured, probe_field):
    groups = 4
    dma = pltpu.SemaphoreType.DMA
    anywhere = pl.BlockSpec(memory_space=pl.ANY)
    return pl.pallas_call(
        halo_kernel,
        in_specs=[pl.BlockSpec(memory_space=pltpu.HBM)] * 3,
        out_specs=[anywhere] * 3 + [pl.BlockSpec(memory_space=pltpu.VMEM)] * 2,
        out_shape=[jax.ShapeDtypeStruct((2, 6, 4 * RIM, LANES), F32), jax.ShapeDtypeStruct(measured.shape, F32),
                   jax.ShapeDtypeStruct((2, 2, 2 * RIM, LANES), F32), jax.ShapeDtypeStruct((2, 6, 4 * RIM, LANES), F32),
                   jax.ShapeDtypeStruct((2, 2, 2 * RIM, LANES), F32)],
        scratch_shapes=[
            pltpu.VMEM((2, RIM, LANES), F32),
            pltpu.VMEM(measured.shape, F32),
            pltpu.VMEM(measured.shape, F32),
            dma((8,)), dma((8,)), dma((10,)),
            dma((4,)), dma((groups,)), dma((groups,)), dma((8,)), dma((8,)), dma((2,)),
        ],
        compiler_params=pltpu.CompilerParams(collective_id=0, has_side_effects=True, vmem_limit_bytes=16 * 2**20),
        name="halo",
    )(object_field, measured, probe_field)


def gather_kernel(acc_ref, term_ref, own, result, total, *rest):
    (recv_v, recv_in, recv_c, recv_h, recv_d, side, part1, part2, part3,
     load_sem, send_sem, recv_sem, s1, r1, s2, r2, s3, r3, s4, r4, s5, r5, s6, r6) = rest
    p, t = lax.axis_index(POS), lax.axis_index(TILE)
    x, z = p // 4, lax.rem(p, 4)
    y = t // 2
    core, inner, partner = chip_side()
    yz = y * 4 + z
    yes = p >= 0
    x_peers = [(lax.rem(x + k, 4) * 4 + z, t) for k in range(1, 4)]
    x_ids = [lax.rem(x + k, 4) for k in range(1, 4)]
    yz_ids = [lax.rem(yz + k, 16) for k in range(1, 16)]
    yz_peers = [(x * 4 + lax.rem(i, 4), (i // 4) * 2 + core) for i in yz_ids]
    sides = [neighbour(0, -1), neighbour(0, 1)]
    outer, outer_in = neighbour(-inner, 0)
    corners = [neighbour(-inner, -1), neighbour(-inner, 1)]

    load_total = pltpu.make_async_copy(term_ref, total, load_sem.at[0])
    load_own = pltpu.make_async_copy(acc_ref.at[:, pl.ds(1, 4), pl.ds(RIM, 2 * RIM), :], own, load_sem.at[1])
    load_sides = [pltpu.make_async_copy(acc_ref.at[:, b, pl.ds(RIM, 2 * RIM), :], side.at[k], load_sem.at[2 + k])
                  for k, b in enumerate((0, 5))]
    load_total.start()
    for load in load_sides:
        load.start()
    load_own.start()
    greet([(partner, yes), (outer, outer_in)] + sides + corners + [(d, yes) for d in x_peers] + [(d, yes) for d in yz_peers])
    load_total.wait()
    half = 512
    mine = pl.multiple_of(core * half, half)
    other = pl.multiple_of((1 - core) * half, half)
    quarter = half // 4
    order = x_ids + [x]
    firsts = [remote(total.at[pl.ds(pl.multiple_of(other + i * quarter, quarter), quarter)], part1.at[k], s1.at[k], r1.at[k], partner)
              for k, i in enumerate(order)]
    for c in firsts:
        c.start()
    inner_halo = pl.multiple_of((1 - core) * 3 * RIM, RIM)
    outer_halo = pl.multiple_of(core * 3 * RIM, RIM)
    count = 0

    def link(src, dst, device):
        nonlocal count
        copy = remote(src, dst, send_sem.at[count], recv_sem.at[count], device)
        count += 1
        return copy

    inner_corners = [link(acc_ref.at[:, b, pl.ds(inner_halo, RIM), :], recv_c.at[k], partner) for k, b in enumerate((0, 5))]
    for copy in inner_corners:
        copy.start()
    inner_main = link(acc_ref.at[:, pl.ds(1, 4), pl.ds(inner_halo, RIM), :], recv_in, partner)
    outer_main = link(acc_ref.at[:, pl.ds(1, 4), pl.ds(outer_halo, RIM), :], recv_v, outer)
    diagonal = [link(acc_ref.at[:, b, pl.ds(outer_halo, RIM), :], recv_d.at[k], corners[k][0]) for k, b in enumerate((0, 5))]
    across = [link(side.at[k], recv_h.at[k], sides[k][0]) for k in range(2)]
    when_each(outer_in, outer_main.start)
    seconds = []
    for k, i in enumerate(order):
        firsts[k].wait_recv()
        rows = pl.ds(pl.multiple_of(mine + i * quarter, quarter), quarter)
        total[rows] = total[rows] + part1[k]
        if k < 3:
            seconds.append(remote(total.at[rows], part2.at[k], s2.at[k], r2.at[k], x_peers[k]))
            seconds[k].start()
    inner_main.start()
    near = pl.multiple_of((1 - core) * RIM, RIM)
    for k in range(2):
        inner_corners[k].wait()
        load_sides[k].wait()
        side[k, :, pl.ds(near, RIM), :] = side[k, :, pl.ds(near, RIM), :] + recv_c[k]
        when_each(sides[k][1], across[k].start)
    at2 = pl.multiple_of(mine + x * quarter, quarter)
    for c in seconds:
        c.wait_recv()
    total[pl.ds(at2, quarter)] = total[pl.ds(at2, quarter)] + part2[0] + part2[1] + part2[2]
    piece = quarter // 16
    thirds = [remote(total.at[pl.ds(pl.multiple_of(at2 + i * piece, piece), piece)], part3.at[k], s3.at[k], r3.at[k], d)
              for k, (i, d) in enumerate(zip(yz_ids, yz_peers))]
    for c in thirds:
        c.start()
    load_own.wait()
    far = pl.multiple_of(core * RIM, RIM)
    inner_main.wait()

    def add_rows(src, at):
        def body(i, carry):
            plane, b = i // 4, lax.rem(i, 4)
            own[plane, b, pl.ds(at, RIM), :] = own[plane, b, pl.ds(at, RIM), :] + src[plane, b]
            return carry
        lax.fori_loop(0, 8, body, 0)

    add_rows(recv_in, near)
    for c in thirds:
        c.wait_recv()
    at3 = pl.multiple_of(at2 + yz * piece, piece)
    value = total[pl.ds(at3, piece)]
    for k in range(15):
        value = value + part3[k]
    result[pl.ds(at3, piece)] = value * (1.0 / math.sqrt(2048))
    here = result.at[pl.ds(at3, piece)]
    fourths = [remote(here, here, s4.at[k], r4.at[k], d) for k, d in enumerate(yz_peers)]
    for c in fourths:
        c.start()

    @pl.when(outer_in)
    def _():
        outer_main.wait()
        add_rows(recv_v, far)

    for c in fourths:
        c.wait_recv()
    here2 = result.at[pl.ds(at2, quarter)]
    fifths = [remote(here2, here2, s5.at[k], r5.at[k], d) for k, d in enumerate(x_peers)]
    for c in fifths:
        c.start()
    lasts = [remote(here2, here2, s6.at[3], r6.at[3], partner)]
    lasts[0].start()
    for k in range(2):
        when_each(corners[k][1], diagonal[k].start)
    for k in range(2):
        block = 3 - 3 * k
        source, diagonal_source = sides[1 - k][1], corners[1 - k][1]

        @pl.when(source)
        def _():
            across[k].wait_recv()
            own[:, block] = own[:, block] + recv_h[k]

        @pl.when(diagonal_source)
        def _():
            diagonal[k].wait_recv()
            own[:, block, pl.ds(far, RIM), :] = own[:, block, pl.ds(far, RIM), :] + recv_d[k]
    for k, c in enumerate(fifths):
        c.wait_recv()
        from_x = lax.rem(x + 3 - k, 4)
        here1 = result.at[pl.ds(pl.multiple_of(mine + from_x * quarter, quarter), quarter)]
        lasts.append(remote(here1, here1, s6.at[k], r6.at[k], partner))
        lasts[-1].start()
    for c in lasts:
        c.wait_recv()
    for c in firsts + seconds + thirds + fourths + fifths + lasts:
        c.wait_send()
    for k in range(2):
        when_each(sides[k][1], across[k].wait_send)
        when_each(corners[k][1], diagonal[k].wait_send)


def collect(acc, term):
    dma = pltpu.SemaphoreType.DMA
    vmem = lambda *shape: pltpu.VMEM(shape, F32)
    return pl.pallas_call(
        gather_kernel,
        in_specs=[pl.BlockSpec(memory_space=pl.ANY)] * 2,
        out_specs=[pl.BlockSpec(memory_space=pltpu.VMEM)] * 2,
        out_shape=[jax.ShapeDtypeStruct((2, 4, 2 * RIM, LANES), F32), jax.ShapeDtypeStruct((1024, LANES), F32)],
        scratch_shapes=[
            vmem(1024, LANES),
            vmem(2, 4, RIM, LANES), vmem(2, 4, RIM, LANES), vmem(2, 2, RIM, LANES), vmem(2, 2, 2 * RIM, LANES),
            vmem(2, 2, RIM, LANES), vmem(2, 2, 2 * RIM, LANES),
            vmem(4, 128, LANES), vmem(3, 128, LANES), vmem(15, 8, LANES),
            dma((4,)), dma((8,)), dma((8,)), dma((4,)), dma((4,)), dma((3,)), dma((3,)), dma((15,)), dma((15,)),
            dma((15,)), dma((15,)), dma((3,)), dma((3,)), dma((4,)), dma((4,)),
        ],
        compiler_params=pltpu.CompilerParams(collective_id=1, has_side_effects=True, vmem_limit_bytes=16 * 2**20),
        name="collect",
    )(acc, term.reshape(1024, LANES))


def layout_kernel(own_ref, sum_ref, obj_ref, probe_ref, sem):
    copies = [pltpu.make_async_copy(own_ref.at[:, b], obj_ref.at[:, :, pl.ds(b * LANES, LANES)], sem.at[b]) for b in range(4)]
    copies += [pltpu.make_async_copy(sum_ref.at[i // 2, i % 2], probe_ref.at[i // 2, :, pl.ds((i % 2) * LANES, LANES)], sem.at[4 + i])
               for i in range(4)]
    for copy in copies:
        copy.start()
    for copy in copies:
        copy.wait()


def laid_out(own, probe_sum):
    return pl.pallas_call(
        layout_kernel,
        in_specs=[pl.BlockSpec(memory_space=pltpu.VMEM)] * 2,
        out_specs=[pl.BlockSpec(memory_space=pl.ANY)] * 2,
        out_shape=[jax.ShapeDtypeStruct((2, 2 * RIM, 4 * LANES), F32), jax.ShapeDtypeStruct((2, 2 * RIM, 2 * LANES), F32)],
        scratch_shapes=[pltpu.SemaphoreType.DMA((8,))],
        compiler_params=pltpu.CompilerParams(vmem_limit_bytes=4 * 2**20),
        name="layout",
    )(own, probe_sum.reshape(2, 2, 2 * RIM, LANES))


def on_device(object_field, probe_field, measured, offsets):
    fixed = [pltpu.with_memory_space_constraint(a, pltpu.HBM) for a in (object_field, measured, probe_field)]
    ext, ordered, probe, acc, term = exchange(*fixed)
    acc, term = compute(offsets.T, ext, probe, ordered, jnp.asarray(dft_tables(256)), jnp.asarray(row_tables(256)), acc, term)
    return tuple(laid_out(*collect(acc, term)))


def solution(mesh):
    placed = (P(None, "tile", "pos"), P(), P(("pos", "tile"), None, None), P(("pos", "tile"), None))
    return jax.shard_map(
        on_device,
        mesh=mesh,
        in_specs=placed,
        out_specs=(P(None, "tile", "pos"), P()),
        check_vma=False,
    )
```
